32 devices in a mesh: dp: 8 (over z, core), tp: 4 (over y, x).
Axes of the slice: x: 2, y: 2, z: 4, core: 2. Of those that a mesh axis runs over, the one named last changes fastest.
Arguments:
- tokens: bfloat16 [1024, 2048], P(('dp', 'tp')), may hold values from -6 to 6
- norm_gain: float32 [2048], replicated, may hold values from 0.5 to 1.5
- w_query: bfloat16 [2048, 2048], P('dp', 'tp'), may hold values from -0.125 to 0.125
- w_key: bfloat16 [2048, 2048], P('dp', 'tp'), may hold values from -0.125 to 0.125
- w_value: bfloat16 [2048, 4096], P('dp', 'tp'), may hold values from -0.125 to 0.125
- w_gate: bfloat16 [2048, 4096], P('dp', 'tp'), may hold values from -0.125 to 0.125
- w_beta: bfloat16 [2048, 32], P('dp', 'tp'), may hold values from -0.125 to 0.125
- w_decay: bfloat16 [2048, 32], P('dp', 'tp'), may hold values from -0.125 to 0.125
- conv_query: float32 [4, 2048], P(None, 'tp'), may hold values from -3 to 3
- conv_key: float32 [4, 2048], P(None, 'tp'), may hold values from -3 to 3
- conv_value: float32 [4, 4096], P(None, 'tp'), may hold values from -3 to 3
- decay_rate: float32 [32], P('tp'), may hold values from 0.004 to 0.04
- dt_bias: float32 [32], P('tp'), may hold values from -1 to 1
- out_gain: float32 [128], replicated, may hold values from 0.5 to 1.5
- seg_ids: int32 [8, 128], P('dp'), may hold values from 0 to 15, never falling along the last dimension, each value on 1 to 32 neighbouring positions
Outputs:
- mixed_tiles: bfloat16 [1024, 4096], P(('dp', 'tp'))
The draws below stay inside these ranges and needn't reach their ends.
Inputs may be any that keep to these rules, and one draw needn't show every extreme that they name: Each row of seg_ids never falls; every prompt covers 1 to 32 consecutive positions.
All inputs are finite; a program needn't handle non-finite values.
Results may differ from the reference program's by a relative error of at most 0.0034.
The reference program's roundings to bfloat16 on the way (of `normed`) count: a program that leaves them out, or rounds other values in their place, can miss the bound.
Values may be sent and summed in bfloat16 or wider, within the bound.
A program may use at most 64 MiB of HBM per device.

```python
import math
import jax
import jax.numpy as jnp
import numpy as np
from jax import lax

D = 2048
KH = 16
VH = 32
DK = 128
DV = 128
CONV_K = 4
SPAN = 64
SEGS = 16
ROWS = 128
TOKENS = 1024
N_DP = 8


def shard_levels(key, extent, cuts, low, high):
    def one(axis_at, blocks):
        draws = jax.random.uniform(jax.random.fold_in(jax.random.fold_in(key, 6), axis_at), (blocks,), jnp.float32, low / len(cuts), high / len(cuts))
        return jnp.repeat(jnp.exp(draws), extent[axis_at] // blocks).reshape((-1,) + (1,) * (len(extent) - axis_at - 1))

    level = one(*cuts[0])
    for cut in cuts[1:]:
        level = level * one(*cut)
    return level


def profile(amount, total, most, lean):
    portions = [(1 << 20) // math.isqrt(grade ** lean) + 1 for grade in range(2, amount + 1)]
    spare, given = total - most - (amount - 1), [1] * (amount - 1)
    while spare > 0:
        candidates = [i for i in range(amount - 1) if given[i] < most]
        pool, budget = sum([portions[i] for i in candidates]), spare
        for i in candidates:
            addition = min(most - given[i], max(1, budget * portions[i] // pool), spare)
            given[i] = given[i] + addition
            spare = spare - addition
    return np.array([most] + given)


def uneven(rng, number_of, total, most, slope):
    if number_of == 2:
        one = jax.random.randint(rng, (), max(1, total - most), min(most, total - 1) + 1)
        return jnp.stack([one, total - one])
    lengths = jnp.asarray(profile(number_of, total, most, slope), jnp.int32)
    couples = (number_of - 1) // 2
    donor, taker = lengths[1:1 + 2 * couples:2], lengths[2:2 + 2 * couples:2]
    slack = jnp.minimum(donor - 1, most - taker)
    moved = jax.random.randint(jax.random.fold_in(rng, 1), (couples,), 0, 1 << 20) % (slack + 1)
    lengths = lengths.at[1:1 + 2 * couples:2].set(donor - moved).at[2:2 + 2 * couples:2].set(taker + moved)
    return lengths[jax.random.permutation(jax.random.fold_in(rng, 2), number_of)]


def normal_values(own_key, dims, deviation, limit, cuts=(), kind=jnp.bfloat16):
    loudness = shard_levels(own_key, dims, cuts, -0.22, 0.18) if cuts else 1.0
    array = jax.random.normal(own_key, dims, jnp.float32) * deviation * loudness
    return jnp.minimum(jnp.maximum(array, -limit), limit).astype(kind)


def setup_inputs(seed: int = 0) -> dict:
    streams_of = jax.random.split(jax.random.key(seed), 16)
    tokens = normal_values(streams_of[0], (TOKENS, D), 1.0, 6.0, ((0, 32),))
    norm_gain = jnp.clip(1.0 + 0.1 * jax.random.normal(streams_of[1], (D,), jnp.float32), 0.5, 1.5)
    w_query = normal_values(streams_of[2], (D, KH * DK), D ** -0.5, 0.125, ((0, 8), (1, 4)))
    w_key = normal_values(streams_of[3], (D, KH * DK), D ** -0.5, 0.125, ((0, 8), (1, 4)))
    w_value = normal_values(streams_of[4], (D, VH * DV), D ** -0.5, 0.125, ((0, 8), (1, 4)))
    w_gate = normal_values(streams_of[5], (D, VH * DV), D ** -0.5, 0.125, ((0, 8), (1, 4)))
    w_beta = normal_values(streams_of[6], (D, VH), D ** -0.5, 0.125, ((0, 8), (1, 4)))
    w_decay = normal_values(streams_of[7], (D, VH), D ** -0.5, 0.125, ((0, 8), (1, 4)))
    conv_query = normal_values(streams_of[8], (CONV_K, KH * DK), 0.5, 3.0, ((1, 4),), jnp.float32)
    conv_key = normal_values(streams_of[9], (CONV_K, KH * DK), 0.5, 3.0, ((1, 4),), jnp.float32)
    conv_value = normal_values(streams_of[10], (CONV_K, VH * DV), 0.5, 3.0, ((1, 4),), jnp.float32)
    decay_rate = jnp.clip(jnp.exp(math.log(0.04) - 2.30258502 * jax.random.uniform(streams_of[11], (VH,), jnp.float32) ** shard_levels(streams_of[11], (VH,), ((0, 4),), -0.2, 0.2)), 0.004, 0.04)
    dt_bias = jnp.clip(jax.random.uniform(streams_of[12], (VH,), jnp.float32, -1.0, 1.0) * shard_levels(streams_of[12], (VH,), ((0, 4),), -0.4, 0.0), -1.0, 1.0)
    out_gain = jnp.clip(1.0 + 0.1 * jax.random.normal(streams_of[13], (DV,), jnp.float32), 0.5, 1.5)
    seg_ids = jax.vmap(lambda own: jnp.searchsorted(jnp.cumsum(uneven(own, SEGS, ROWS, ROWS // 4, 2)), jnp.arange(ROWS), side="right"))(jax.random.split(streams_of[14], N_DP)).reshape((N_DP, ROWS)).astype(jnp.int32)
    return {"tokens": tokens, "norm_gain": norm_gain, "w_query": w_query, "w_key": w_key, "w_value": w_value, "w_gate": w_gate, "w_beta": w_beta, "w_decay": w_decay, "conv_query": conv_query, "conv_key": conv_key, "conv_value": conv_value, "decay_rate": decay_rate, "dt_bias": dt_bias, "out_gain": out_gain, "seg_ids": seg_ids}


highest = lax.Precision.HIGHEST

def rms_rows(tokens, gain):
    floats = tokens.astype(jnp.float32)
    scaled = floats * lax.rsqrt(lax.optimization_barrier(jnp.mean(floats * floats, axis=-1, keepdims=True)) + 1e-06)
    return (scaled * gain).astype(jnp.bfloat16)

def split_columns(projected, column_counts):
    pieces = []
    offset = 0
    for count in column_counts:
        pieces.append(projected[:, offset:offset + count])
        offset = offset + count
    return pieces

def causal_conv(projected, kernel, segment):
    kernel_len = kernel.shape[0]
    summed = projected * kernel[kernel_len - 1]
    for offset in range(1, kernel_len):
        zeros_top = jnp.zeros((offset, projected.shape[1]), jnp.float32)
        shifted = jnp.concatenate([zeros_top, projected[:-offset]], axis=0)
        earlier = jnp.concatenate([jnp.full((offset,), -1, jnp.int32), segment[:-offset]])
        same_doc = (earlier == segment).astype(jnp.float32)
        summed = summed + shifted * same_doc[:, None] * kernel[kernel_len - 1 - offset]
    return jax.nn.silu(summed)

def unit_heads(values, heads, head_size):
    shaped = values.reshape(values.shape[0], heads, head_size)
    return shaped * lax.rsqrt(lax.optimization_barrier(jnp.sum(shaped * shaped, axis=-1, keepdims=True)) + 1e-06)

def delta_head(query, key_rows, value, beta, log_decay, segment):
    row_count = query.shape[0]
    blocks = row_count // SPAN
    value_size = value.shape[1]
    q_blocks = query.reshape(blocks, SPAN, query.shape[1])
    k_blocks = key_rows.reshape(blocks, SPAN, key_rows.shape[1])
    v_blocks = value.reshape(blocks, SPAN, value_size)
    beta_blocks = beta.reshape(blocks, SPAN)
    decay_blocks = log_decay.reshape(blocks, SPAN)
    seg_blocks = segment.reshape(blocks, SPAN)
    before = jnp.concatenate([jnp.full((1,), -1, jnp.int32), seg_blocks[:-1, -1]])
    row_index = lax.broadcasted_iota(jnp.int32, (SPAN, SPAN), 0)
    col_index = lax.broadcasted_iota(jnp.int32, (SPAN, SPAN), 1)
    lower_mask = row_index >= col_index
    strict = row_index > col_index

    def advance(state, inputs):
        block_q, block_k, block_v, block_beta, block_decay, block_seg, block_before = inputs
        cumulative = jnp.cumsum(block_decay)
        same_doc = block_seg[:, None] == block_seg[None, :]
        spread = jnp.where(lower_mask, cumulative[:, None] - cumulative[None, :], 0.0)
        decay_matrix = jnp.where(lower_mask & same_doc, jnp.exp(spread), 0.0)
        carried = (block_seg == block_before).astype(jnp.float32)
        from_start = jnp.exp(cumulative) * carried
        key_gram = jnp.dot(block_k, block_k.T, precision=highest)
        lower_matrix = jnp.where(strict, block_beta[:, None] * key_gram * decay_matrix, 0.0)
        system = jnp.eye(SPAN, dtype=jnp.float32) + lower_matrix
        right_side = jnp.concatenate([block_beta[:, None] * block_v, (block_beta * from_start)[:, None] * block_k], axis=1)
        solved = lax.linalg.triangular_solve(system, right_side, left_side=True, lower=True, unit_diagonal=True)
        updates = solved[:, :value_size] - jnp.dot(solved[:, value_size:], state, precision=highest)
        scores = jnp.dot(block_q, block_k.T, precision=highest) * decay_matrix
        output = jnp.dot(from_start[:, None] * block_q, state, precision=highest) + jnp.dot(scores, updates, precision=highest)
        tail_weight = jnp.where(block_seg == block_seg[-1], jnp.exp(cumulative[-1] - cumulative), 0.0)
        new_state = jnp.exp(cumulative[-1]) * carried[-1] * state + jnp.dot((tail_weight[:, None] * block_k).T, updates, precision=highest)
        return (new_state, output)
    initial = jnp.zeros((key_rows.shape[1], value_size), jnp.float32)
    last_state, outputs = lax.scan(advance, initial, (q_blocks, k_blocks, v_blocks, beta_blocks, decay_blocks, seg_blocks, before))
    return outputs.reshape(row_count, value_size)

def mix_rows(parts, segment, conv_query, conv_key, conv_value, decay_rate, dt_bias, out_gain):
    proj_query, proj_key, proj_value, proj_gate, proj_beta, proj_decay = [piece_part.astype(jnp.float32) for piece_part in parts]
    key_heads = proj_query.shape[1] // DK
    value_heads = proj_value.shape[1] // DV
    repeat = value_heads // key_heads
    query = unit_heads(causal_conv(proj_query, conv_query, segment), key_heads, DK) * DK ** (-0.5)
    keys = unit_heads(causal_conv(proj_key, conv_key, segment), key_heads, DK)
    values = causal_conv(proj_value, conv_value, segment).reshape(proj_value.shape[0], value_heads, DV)
    query = jnp.repeat(query, repeat, axis=1)
    keys = jnp.repeat(keys, repeat, axis=1)
    beta = jax.nn.sigmoid(proj_beta)
    log_decay = -decay_rate * jax.nn.softplus(proj_decay + dt_bias)
    mixed = jax.vmap(delta_head, in_axes=(1, 1, 1, 1, 1, None), out_axes=1)(query, keys, values, beta, log_decay, segment)
    normed = mixed * lax.rsqrt(lax.optimization_barrier(jnp.mean(mixed * mixed, axis=-1, keepdims=True)) + 1e-06) * out_gain
    gated = normed * jax.nn.silu(proj_gate.reshape(proj_gate.shape[0], value_heads, DV))
    return gated.reshape(gated.shape[0], value_heads * DV).astype(jnp.bfloat16)

def reference(tokens, norm_gain, w_query, w_key, w_value, w_gate, w_beta, w_decay, conv_query, conv_key, conv_value, decay_rate, dt_bias, out_gain, seg_ids):
    weights = [w_query, w_key, w_value, w_gate, w_beta, w_decay]
    column_counts = [matrix.shape[1] for matrix in weights]
    joined = jnp.concatenate(weights, axis=1)
    groups = tokens.reshape(N_DP, ROWS, D)

    def one_group(operands):
        group_rows, segment = operands
        projected = jnp.dot(rms_rows(group_rows, norm_gain).astype(jnp.float32), joined.astype(jnp.float32), preferred_element_type=jnp.float32).astype(jnp.bfloat16)
        parts = split_columns(projected, column_counts)
        return mix_rows(parts, segment, conv_query, conv_key, conv_value, decay_rate, dt_bias, out_gain)
    mixed = lax.map(one_group, (groups, seg_ids))
    return mixed.reshape(TOKENS, VH * DV)
```

```python
import functools

import jax
import jax.numpy as jnp
from jax import lax
from jax.experimental import pallas as pl
from jax.experimental.pallas import tpu as pltpu
from jax.sharding import PartitionSpec as P

DK = 128
DV = 128
SPAN = 64


highest = lax.Precision.HIGHEST


def rms_rows(tokens, gain):
    floats = tokens.astype(jnp.float32)
    scaled = floats * lax.rsqrt(jnp.mean(floats * floats, axis=-1, keepdims=True) + 1e-06)
    return (scaled * gain).astype(jnp.bfloat16)


def split_columns(projected, column_counts):
    pieces = []
    offset = 0
    for count in column_counts:
        pieces.append(projected[:, offset : offset + count])
        offset = offset + count
    return pieces


def causal_conv(projected, kernel, segment):
    kernel_len = kernel.shape[0]
    summed = projected * kernel[kernel_len - 1]
    for offset in range(1, kernel_len):
        zeros_top = jnp.zeros((offset, projected.shape[1]), jnp.float32)
        shifted = jnp.concatenate([zeros_top, projected[:-offset]], axis=0)
        earlier = jnp.concatenate([jnp.full((offset,), -1, jnp.int32), segment[:-offset]])
        same_doc = (earlier == segment).astype(jnp.float32)
        summed = summed + shifted * same_doc[:, None] * kernel[kernel_len - 1 - offset]
    return jax.nn.silu(summed)


def unit_heads(values, heads, head_size):
    shaped = values.reshape(values.shape[0], heads, head_size)
    return shaped * lax.rsqrt(jnp.sum(shaped * shaped, axis=-1, keepdims=True) + 1e-06)


def delta_head(query, key_rows, value, beta, log_decay, segment):
    row_count = query.shape[0]
    blocks = row_count // SPAN
    value_size = value.shape[1]
    q_blocks = query.reshape(blocks, SPAN, query.shape[1])
    k_blocks = key_rows.reshape(blocks, SPAN, key_rows.shape[1])
    v_blocks = value.reshape(blocks, SPAN, value_size)
    beta_blocks = beta.reshape(blocks, SPAN)
    decay_blocks = log_decay.reshape(blocks, SPAN)
    seg_blocks = segment.reshape(blocks, SPAN)
    before = jnp.concatenate([jnp.full((1,), -1, jnp.int32), seg_blocks[:-1, -1]])
    row_index = lax.broadcasted_iota(jnp.int32, (SPAN, SPAN), 0)
    col_index = lax.broadcasted_iota(jnp.int32, (SPAN, SPAN), 1)
    lower_mask = row_index >= col_index
    strict = row_index > col_index

    def advance(state, inputs):
        block_q, block_k, block_v, block_beta, block_decay, block_seg, block_before = inputs
        cumulative = jnp.cumsum(block_decay)
        same_doc = block_seg[:, None] == block_seg[None, :]
        spread = jnp.where(lower_mask, cumulative[:, None] - cumulative[None, :], 0.0)
        decay_matrix = jnp.where(lower_mask & same_doc, jnp.exp(spread), 0.0)
        carried = (block_seg == block_before).astype(jnp.float32)
        from_start = jnp.exp(cumulative) * carried
        key_gram = jnp.dot(block_k, block_k.T, precision=highest)
        lower_matrix = jnp.where(strict, block_beta[:, None] * key_gram * decay_matrix, 0.0)
        system = jnp.eye(SPAN, dtype=jnp.float32) + lower_matrix
        right_side = jnp.concatenate(
            [block_beta[:, None] * block_v, (block_beta * from_start)[:, None] * block_k], axis=1
        )
        solved = lax.linalg.triangular_solve(
            system, right_side, left_side=True, lower=True, unit_diagonal=True
        )
        updates = solved[:, :value_size] - jnp.dot(solved[:, value_size:], state, precision=highest)
        scores = jnp.dot(block_q, block_k.T, precision=highest) * decay_matrix
        output = jnp.dot(from_start[:, None] * block_q, state, precision=highest) + jnp.dot(
            scores, updates, precision=highest
        )
        tail_weight = jnp.where(
            block_seg == block_seg[-1], jnp.exp(cumulative[-1] - cumulative), 0.0
        )
        new_state = jnp.exp(cumulative[-1]) * carried[-1] * state + jnp.dot(
            (tail_weight[:, None] * block_k).T, updates, precision=highest
        )
        return (new_state, output)

    initial = jnp.zeros((key_rows.shape[1], value_size), jnp.float32)
    last_state, outputs = lax.scan(
        advance,
        initial,
        (q_blocks, k_blocks, v_blocks, beta_blocks, decay_blocks, seg_blocks, before),
    )
    return outputs.reshape(row_count, value_size)


def prepare_heads(parts, segment, conv_query, conv_key, conv_value, decay_rate, dt_bias):
    proj_query, proj_key, proj_value, proj_gate, proj_beta, proj_decay = [
        piece_part.astype(jnp.float32) for piece_part in parts
    ]
    key_heads = proj_query.shape[1] // DK
    value_heads = proj_value.shape[1] // DV
    repeat = value_heads // key_heads
    query = unit_heads(causal_conv(proj_query, conv_query, segment), key_heads, DK) * DK ** (-0.5)
    keys = unit_heads(causal_conv(proj_key, conv_key, segment), key_heads, DK)
    values = causal_conv(proj_value, conv_value, segment).reshape(
        proj_value.shape[0], value_heads, DV
    )
    query = jnp.repeat(query, repeat, axis=1)
    keys = jnp.repeat(keys, repeat, axis=1)
    beta = jax.nn.sigmoid(proj_beta)
    log_decay = -decay_rate * jax.nn.softplus(proj_decay + dt_bias)
    gate_act = jax.nn.silu(proj_gate.reshape(proj_gate.shape[0], value_heads, DV))
    return (query, keys, values, beta, log_decay, gate_act)


def finish_heads(mixed, gate_act, out_gain):
    normed = mixed * lax.rsqrt(jnp.mean(mixed * mixed, axis=-1, keepdims=True) + 1e-06) * out_gain
    return (normed * gate_act).astype(jnp.bfloat16)


def shards(
    tokens,
    norm_gain,
    w_query,
    w_key,
    w_value,
    w_gate,
    w_beta,
    w_decay,
    conv_query,
    conv_key,
    conv_value,
    decay_rate,
    dt_bias,
    out_gain,
    seg_ids,
):
    gathered = (
        lax.all_gather(w_query, "dp", axis=0, tiled=True),
        lax.all_gather(w_key, "dp", axis=0, tiled=True),
        lax.all_gather(w_value, "dp", axis=0, tiled=True),
        lax.all_gather(w_gate, "dp", axis=0, tiled=True),
        lax.all_gather(w_beta, "dp", axis=0, tiled=True),
        lax.all_gather(w_decay, "dp", axis=0, tiled=True),
    )
    column_counts = [matrix.shape[1] for matrix in gathered]
    joined = jnp.concatenate(gathered, axis=1)
    projected = jnp.dot(
        rms_rows(lax.all_gather(tokens, "tp", axis=0, tiled=True), norm_gain),
        joined,
        preferred_element_type=jnp.float32,
    ).astype(jnp.bfloat16)
    parts = split_columns(projected, column_counts)
    segment = seg_ids[0]
    query, keys, values, beta, log_decay, gate_act = prepare_heads(
        parts, segment, conv_query, conv_key, conv_value, decay_rate, dt_bias
    )
    row_count = values.shape[0]
    local_heads = values.shape[1]
    mixed = jax.vmap(delta_head, in_axes=(1, 1, 1, 1, 1, None), out_axes=1)(
        query, keys, values, beta, log_decay, segment
    )
    tiles = finish_heads(mixed, gate_act, out_gain).reshape(row_count, local_heads * DV)
    return lax.all_to_all(tiles, "tp", split_axis=0, concat_axis=1, tiled=True)


MESH = pl.DeviceIdType.MESH
CORES = 2
STEP = 8


def dot_exact(left, right):
    return jnp.dot(left, right, precision=highest, preferred_element_type=jnp.float32)


def dot_rows(left, right, precision=None):
    return lax.dot_general(
        left,
        right,
        (((1,), (1,)), ((), ())),
        precision=precision,
        preferred_element_type=jnp.float32,
    )


def sigmoid(x):
    return 1.0 / (1.0 + jnp.exp(-x))


def unit_rows(values):
    return values * lax.rsqrt(jnp.sum(values * values, axis=-1, keepdims=True) + 1e-06)


def conv_rows(projected, taps, same_before):
    summed = projected * taps[3:4]
    for offset in range(1, 4):
        shifted = pltpu.roll(projected, offset, 0)
        mask = same_before[offset - 1]
        if projected.shape[1] > mask.shape[1]:
            mask = jnp.concatenate([mask] * (projected.shape[1] // mask.shape[1]), axis=1)
        summed = summed + jnp.where(mask, shifted, 0.0) * taps[3 - offset : 4 - offset]
    return summed * sigmoid(summed)


def mix_groups(z, nz, heads, tok, weights, ba, seg, taps_q, taps_k, taps_v, rate, bias, gain, out):
    rows = seg.shape[2]
    row = lax.broadcasted_iota(jnp.int32, (rows, rows), 0)
    col = lax.broadcasted_iota(jnp.int32, (rows, rows), 1)
    lower = row >= col
    strict = row > col
    eye = jnp.where(row == col, 1.0, 0.0)
    ones_lower = jnp.where(lower, 1.0, 0.0)
    width = heads * DV
    count = rate.shape[1]
    lane = lax.broadcasted_iota(jnp.int32, (rows, count), 1)
    tq = taps_q[:, pl.ds(pl.multiple_of(z * DK, DK), DK)]
    tk = taps_k[:, pl.ds(pl.multiple_of(z * DK, DK), DK)]
    tv = taps_v[:, pl.ds(pl.multiple_of(z * width, width), width)]
    sources, depth = weights.shape[0], weights.shape[1]

    def block(size):
        return row // size == col // size

    chains = []
    gates = []
    for g in range(nz):
        rows_g = tok[g].reshape(rows, tok.shape[3])
        full = weights[...].reshape(sources * depth, weights.shape[2])
        projected = jnp.dot(rows_g, full, preferred_element_type=jnp.float32)
        projected = projected.astype(jnp.bfloat16).astype(jnp.float32)
        small = jnp.zeros((rows, ba.shape[1]), jnp.float32)
        for s in range(sources):
            small = small + dot_rows(rows_g[:, s * depth : (s + 1) * depth], ba[s])
        small = small.astype(jnp.bfloat16).astype(jnp.float32)
        beta_all = sigmoid(small[:, :count])
        shifted = small[:, count : 2 * count] + bias[...]
        soft = jnp.maximum(shifted, 0.0) + jnp.log1p(jnp.exp(-jnp.abs(shifted)))
        cumulative = dot_exact(ones_lower, -rate[...] * soft)
        seg_row = jnp.broadcast_to(seg[g][0:1].astype(jnp.float32), (rows, rows))
        seg_col = seg_row.T
        same = seg_row == seg_col
        same_before = [
            (pltpu.roll(seg_col, offset, 0) == seg_col) & (row >= offset) for offset in range(1, 4)
        ]
        query = unit_rows(conv_rows(projected[:, :DK], tq, same_before)) * DK ** (-0.5)
        key = unit_rows(conv_rows(projected[:, DK : 2 * DK], tk, same_before))
        values = conv_rows(projected[:, 2 * DK : 2 * DK + width], tv, same_before)
        gate = projected[:, 2 * DK + width :]
        key_gram = dot_rows(key, key, highest)
        query_gram = dot_rows(query, key, highest)
        gates.append(gate * sigmoid(gate))
        for h in range(heads):
            pick = lane == z * heads + h
            beta = jnp.sum(jnp.where(pick, beta_all, 0.0), axis=1, keepdims=True)
            total = jnp.sum(jnp.where(pick, cumulative, 0.0), axis=1, keepdims=True)
            total = jnp.broadcast_to(total, (rows, rows))
            spread = jnp.where(lower, total - total.T, 0.0)
            decay = jnp.where(lower & same, jnp.exp(spread), 0.0)
            chains.append(
                (
                    jnp.where(strict, beta * key_gram * decay, 0.0),
                    query_gram * decay,
                    beta * values[:, h * DV : (h + 1) * DV],
                )
            )
    lows = [c[0] for c in chains]
    inner = [jnp.where(block(STEP), m, 0.0) for m in lows]
    squares = [dot_exact(m, m) for m in inner]
    fourths = [dot_exact(m, m) for m in squares]
    firsts = [eye - m + s - dot_exact(m, s) for m, s in zip(inner, squares)]
    inverse = [f + dot_exact(f, q) for f, q in zip(firsts, fourths)]
    size = STEP
    while size < rows // 4:
        ring = block(2 * size) & jnp.logical_not(block(size))
        parts = [dot_exact(jnp.where(ring, m, 0.0), t) for m, t in zip(lows, inverse)]
        inverse = [t - dot_exact(t, p) for t, p in zip(inverse, parts)]
        size = 2 * size
    outer = jnp.logical_not(block(size))
    solved = [dot_exact(t, c[2]) for t, c in zip(inverse, chains)]
    parts = [dot_exact(jnp.where(outer, m, 0.0), x) for m, x in zip(lows, solved)]
    solved = [x - dot_exact(t, p) for x, t, p in zip(solved, inverse, parts)]
    mixed = [dot_exact(c[1], x) for c, x in zip(chains, solved)]
    for g in range(nz):
        for h in range(heads):
            m = mixed[g * heads + h]
            normed = m * lax.rsqrt(jnp.mean(m * m, axis=-1, keepdims=True) + 1e-06) * gain[...]
            tile = (normed * gates[g][:, h * DV : (h + 1) * DV]).astype(jnp.bfloat16)
            for t in range(out.shape[1]):
                share = rows // out.shape[1]
                out[g, t, :, h * DV : (h + 1) * DV] = tile[t * share : (t + 1) * share]


def layer_kernel(
    nz,
    ntp,
    heads,
    tokens,
    norm_gain,
    w_query,
    w_key,
    w_value,
    w_gate,
    w_ba,
    taps_q,
    taps_k,
    taps_v,
    rate,
    bias,
    gain,
    seg_own,
    out,
    tok,
    weights,
    ba,
    seg,
    tiles,
    zs,
    zr,
    ys,
    yr,
    ws,
    wr,
    os,
    orr,
    rs,
    rr,
    bs,
    br,
    brs,
    brr,
    ss,
    sr,
    cs,
    cr,
    local,
):
    dp = lax.axis_index("dp")
    tp = lax.axis_index("tp")
    z = dp // CORES
    core = dp % CORES
    sibling = (z * CORES + 1 - core, tp)
    width = heads * DV

    def z_at(k):
        return lax.rem(z + k, nz)

    def dp_at(k):
        return z_at(k) * CORES + core

    def tp_at(j):
        return lax.rem(tp + j, ntp)

    def remote(source, target, send, recv, device):
        return pltpu.make_async_remote_copy(
            src_ref=source,
            dst_ref=target,
            send_sem=send,
            recv_sem=recv,
            device_id=device,
            device_id_type=MESH,
        )

    barrier = pltpu.get_barrier_semaphore()
    for k in range(nz):
        for j in range(ntp):
            if k or j:
                pl.semaphore_signal(
                    barrier, inc=1, device_id=(dp_at(k), tp_at(j)), device_id_type=MESH
                )
    pl.semaphore_signal(barrier, inc=1, device_id=sibling, device_id_type=MESH)

    floats = tokens[...].astype(jnp.float32)
    scaled = floats * lax.rsqrt(jnp.mean(floats * floats, axis=-1, keepdims=True) + 1e-06)
    tok[z, tp] = (scaled * norm_gain[...]).astype(jnp.bfloat16)
    seg[z] = seg_own[...]
    ba[dp] = w_ba[...]

    def pieces(chip):
        return (
            (w_query.at[:, pl.ds(pl.multiple_of(chip * DK, DK), DK)], 0, DK),
            (w_key.at[:, pl.ds(pl.multiple_of(chip * DK, DK), DK)], DK, DK),
            (w_value.at[:, pl.ds(pl.multiple_of(chip * width, width), width)], 2 * DK, width),
            (w_gate.at[:, pl.ds(pl.multiple_of(chip * width, width), width)], 2 * DK + width, width),
        )

    own_local = []
    for i, (source, start, size) in enumerate(pieces(z)):
        copy = pltpu.make_async_copy(source, weights.at[dp, :, pl.ds(start, size)], local.at[i])
        copy.start()
        own_local.append(copy)

    pl.semaphore_wait(barrier, nz * ntp)

    sends = []
    tok_z = []
    seg_z = []
    ba_z = []
    for k in range(1, nz):
        peer = (dp_at(k), tp)
        copy = remote(tok.at[z, tp], tok.at[z, tp], zs.at[k], zr.at[k], peer)
        copy.start()
        tok_z.append(copy)
        copy = remote(seg.at[z], seg.at[z], ss.at[k], sr.at[k], peer)
        copy.start()
        seg_z.append(copy)
        copy = remote(ba.at[dp], ba.at[dp], bs.at[k], br.at[k], peer)
        copy.start()
        ba_z.append(copy)
    tok_y = []

    def spread_rows(k):
        at = lax.rem(z + nz - k, nz)
        for j in range(1, ntp):
            copy = remote(
                tok.at[at, tp], tok.at[at, tp], ys.at[k, j], yr.at[k, j], (dp, tp_at(j))
            )
            copy.start()
            tok_y.append(copy)

    spread_rows(0)
    weight_z = []
    for k in range(1, nz):
        for i, (source, start, size) in enumerate(pieces(z_at(k))):
            copy = remote(
                source,
                weights.at[dp, :, pl.ds(start, size)],
                ws.at[k, i],
                wr.at[k, i],
                (dp_at(k), tp),
            )
            copy.start()
            weight_z.append(copy)
    own_sibling = []
    for i, (source, start, size) in enumerate(pieces(z)):
        copy = remote(
            source, weights.at[dp, :, pl.ds(start, size)], os.at[i], orr.at[i], sibling
        )
        copy.start()
        own_sibling.append(copy)
    ba_own = remote(ba.at[dp], ba.at[dp], brs.at[0], brr.at[0], sibling)
    ba_own.start()

    for k in range(1, nz):
        tok_z[k - 1].wait_recv()
        spread_rows(k)
    relays = []
    for k in range(1, nz):
        at = lax.rem(z + nz - k, nz) * CORES + core
        ba_z[k - 1].wait_recv()
        copy = remote(ba.at[at], ba.at[at], brs.at[k], brr.at[k], sibling)
        copy.start()
        relays.append(copy)
        for i in range(4):
            weight_z[(k - 1) * 4 + i].wait_recv()
        copy = remote(weights.at[at], weights.at[at], rs.at[k], rr.at[k], sibling)
        copy.start()
        relays.append(copy)
    for copy in own_local:
        copy.wait()
    for copy in tok_z + ba_z + weight_z:
        copy.wait_send()
    for copy in seg_z + tok_y + own_sibling + relays + [ba_own]:
        copy.wait()

    mix_groups(
        z, nz, heads, tok, weights, ba, seg, taps_q, taps_k, taps_v, rate, bias, gain, tiles
    )

    place = pl.ds(pl.multiple_of((tp * nz + z) * width, width), width)
    finals = []
    for k in range(nz):
        for j in range(ntp):
            source = tiles.at[z_at(k), tp_at(j)]
            if k or j:
                copy = remote(
                    source, out.at[:, place], cs.at[k, j], cr.at[k, j], (dp_at(k), tp_at(j))
                )
            else:
                copy = pltpu.make_async_copy(source, out.at[:, place], cs.at[0, 0])
            copy.start()
            finals.append(copy)
    for copy in finals:
        copy.wait()


def layer(n_dp, n_tp, *args):
    (
        tokens,
        norm_gain,
        w_query,
        w_key,
        w_value,
        w_gate,
        w_beta,
        w_decay,
        conv_query,
        conv_key,
        conv_value,
        decay_rate,
        dt_bias,
        out_gain,
        seg_ids,
    ) = args
    nz = n_dp // CORES
    rows = seg_ids.shape[1]
    share, model = tokens.shape
    depth = w_query.shape[0]
    value_heads = w_value.shape[1] // DV
    if n_dp % CORES or w_query.shape[1] // DK != nz or value_heads % nz or rows != 128:
        return shards(*args)
    heads = value_heads // nz
    wide = 2 * DK + 2 * heads * DV
    w_ba = jnp.concatenate([w_beta, w_decay], axis=1).T
    small = w_ba.shape[0]
    vmem = pl.BlockSpec(memory_space=pltpu.VMEM)
    anywhere = pl.BlockSpec(memory_space=pl.ANY)
    dma = pltpu.SemaphoreType.DMA
    return pl.pallas_call(
        functools.partial(layer_kernel, nz, n_tp, heads),
        out_shape=jax.ShapeDtypeStruct((share, n_tp * value_heads * DV), jnp.bfloat16),
        in_specs=[vmem, vmem] + [anywhere] * 4 + [vmem] * 8,
        out_specs=vmem,
        scratch_shapes=[
            pltpu.VMEM((nz, n_tp, share, model), jnp.bfloat16),
            pltpu.VMEM((n_dp, depth, wide), jnp.bfloat16),
            pltpu.VMEM((n_dp, small, depth), jnp.bfloat16),
            pltpu.VMEM((nz, 8, rows), jnp.int32),
            pltpu.VMEM((nz, n_tp, share, heads * DV), jnp.bfloat16),
            dma((nz,)),
            dma((nz,)),
            dma((nz, n_tp)),
            dma((nz, n_tp)),
            dma((nz, 4)),
            dma((nz, 4)),
            dma((4,)),
            dma((4,)),
            dma((nz,)),
            dma((nz,)),
            dma((nz,)),
            dma((nz,)),
            dma((nz,)),
            dma((nz,)),
            dma((nz,)),
            dma((nz,)),
            dma((nz, n_tp)),
            dma((nz, n_tp)),
            dma((4,)),
        ],
        compiler_params=pltpu.CompilerParams(
            collective_id=0, has_side_effects=True, vmem_limit_bytes=48 * 2**20
        ),
    )(
        tokens,
        norm_gain.reshape(1, -1),
        w_query,
        w_key,
        w_value,
        w_gate,
        w_ba,
        conv_query,
        conv_key,
        conv_value,
        decay_rate.reshape(1, -1),
        dt_bias.reshape(1, -1),
        out_gain.reshape(1, -1),
        jnp.broadcast_to(seg_ids, (8, rows)),
    )


def solution(mesh):
    in_specs = (
        P(("dp", "tp"), None),
        P(),
        P("dp", "tp"),
        P("dp", "tp"),
        P("dp", "tp"),
        P("dp", "tp"),
        P("dp", "tp"),
        P("dp", "tp"),
        P(None, "tp"),
        P(None, "tp"),
        P(None, "tp"),
        P("tp"),
        P("tp"),
        P(),
        P("dp", None),
    )
    out_specs = P(("dp", "tp"), None)
    body = functools.partial(layer, mesh.shape["dp"], mesh.shape["tp"])
    return jax.shard_map(body, mesh=mesh, in_specs=in_specs, out_specs=out_specs, check_vma=False)
```

```python
import functools

import jax
import jax.numpy as jnp
from jax import lax
from jax.experimental import pallas as pl
from jax.experimental.pallas import tpu as pltpu
from jax.sharding import PartitionSpec as P

DK = 128
DV = 128
SPAN = 64


highest = lax.Precision.HIGHEST


def rms_rows(tokens, gain):
    floats = tokens.astype(jnp.float32)
    scaled = floats * lax.rsqrt(jnp.mean(floats * floats, axis=-1, keepdims=True) + 1e-06)
    return (scaled * gain).astype(jnp.bfloat16)


def split_columns(projected, column_counts):
    pieces = []
    offset = 0
    for count in column_counts:
        pieces.append(projected[:, offset : offset + count])
        offset = offset + count
    return pieces


def causal_conv(projected, kernel, segment):
    kernel_len = kernel.shape[0]
    summed = projected * kernel[kernel_len - 1]
    for offset in range(1, kernel_len):
        zeros_top = jnp.zeros((offset, projected.shape[1]), jnp.float32)
        shifted = jnp.concatenate([zeros_top, projected[:-offset]], axis=0)
        earlier = jnp.concatenate([jnp.full((offset,), -1, jnp.int32), segment[:-offset]])
        same_doc = (earlier == segment).astype(jnp.float32)
        summed = summed + shifted * same_doc[:, None] * kernel[kernel_len - 1 - offset]
    return jax.nn.silu(summed)


def unit_heads(values, heads, head_size):
    shaped = values.reshape(values.shape[0], heads, head_size)
    return shaped * lax.rsqrt(jnp.sum(shaped * shaped, axis=-1, keepdims=True) + 1e-06)


def delta_head(query, key_rows, value, beta, log_decay, segment):
    row_count = query.shape[0]
    blocks = row_count // SPAN
    value_size = value.shape[1]
    q_blocks = query.reshape(blocks, SPAN, query.shape[1])
    k_blocks = key_rows.reshape(blocks, SPAN, key_rows.shape[1])
    v_blocks = value.reshape(blocks, SPAN, value_size)
    beta_blocks = beta.reshape(blocks, SPAN)
    decay_blocks = log_decay.reshape(blocks, SPAN)
    seg_blocks = segment.reshape(blocks, SPAN)
    before = jnp.concatenate([jnp.full((1,), -1, jnp.int32), seg_blocks[:-1, -1]])
    row_index = lax.broadcasted_iota(jnp.int32, (SPAN, SPAN), 0)
    col_index = lax.broadcasted_iota(jnp.int32, (SPAN, SPAN), 1)
    lower_mask = row_index >= col_index
    strict = row_index > col_index

    def advance(state, inputs):
        block_q, block_k, block_v, block_beta, block_decay, block_seg, block_before = inputs
        cumulative = jnp.cumsum(block_decay)
        same_doc = block_seg[:, None] == block_seg[None, :]
        spread = jnp.where(lower_mask, cumulative[:, None] - cumulative[None, :], 0.0)
        decay_matrix = jnp.where(lower_mask & same_doc, jnp.exp(spread), 0.0)
        carried = (block_seg == block_before).astype(jnp.float32)
        from_start = jnp.exp(cumulative) * carried
        key_gram = jnp.dot(block_k, block_k.T, precision=highest)
        lower_matrix = jnp.where(strict, block_beta[:, None] * key_gram * decay_matrix, 0.0)
        system = jnp.eye(SPAN, dtype=jnp.float32) + lower_matrix
        right_side = jnp.concatenate(
            [block_beta[:, None] * block_v, (block_beta * from_start)[:, None] * block_k], axis=1
        )
        solved = lax.linalg.triangular_solve(
            system, right_side, left_side=True, lower=True, unit_diagonal=True
        )
        updates = solved[:, :value_size] - jnp.dot(solved[:, value_size:], state, precision=highest)
        scores = jnp.dot(block_q, block_k.T, precision=highest) * decay_matrix
        output = jnp.dot(from_start[:, None] * block_q, state, precision=highest) + jnp.dot(
            scores, updates, precision=highest
        )
        tail_weight = jnp.where(
            block_seg == block_seg[-1], jnp.exp(cumulative[-1] - cumulative), 0.0
        )
        new_state = jnp.exp(cumulative[-1]) * carried[-1] * state + jnp.dot(
            (tail_weight[:, None] * block_k).T, updates, precision=highest
        )
        return (new_state, output)

    initial = jnp.zeros((key_rows.shape[1], value_size), jnp.float32)
    last_state, outputs = lax.scan(
        advance,
        initial,
        (q_blocks, k_blocks, v_blocks, beta_blocks, decay_blocks, seg_blocks, before),
    )
    return outputs.reshape(row_count, value_size)


def prepare_heads(parts, segment, conv_query, conv_key, conv_value, decay_rate, dt_bias):
    proj_query, proj_key, proj_value, proj_gate, proj_beta, proj_decay = [
        piece_part.astype(jnp.float32) for piece_part in parts
    ]
    key_heads = proj_query.shape[1] // DK
    value_heads = proj_value.shape[1] // DV
    repeat = value_heads // key_heads
    query = unit_heads(causal_conv(proj_query, conv_query, segment), key_heads, DK) * DK ** (-0.5)
    keys = unit_heads(causal_conv(proj_key, conv_key, segment), key_heads, DK)
    values = causal_conv(proj_value, conv_value, segment).reshape(
        proj_value.shape[0], value_heads, DV
    )
    query = jnp.repeat(query, repeat, axis=1)
    keys = jnp.repeat(keys, repeat, axis=1)
    beta = jax.nn.sigmoid(proj_beta)
    log_decay = -decay_rate * jax.nn.softplus(proj_decay + dt_bias)
    gate_act = jax.nn.silu(proj_gate.reshape(proj_gate.shape[0], value_heads, DV))
    return (query, keys, values, beta, log_decay, gate_act)


def finish_heads(mixed, gate_act, out_gain):
    normed = mixed * lax.rsqrt(jnp.mean(mixed * mixed, axis=-1, keepdims=True) + 1e-06) * out_gain
    return (normed * gate_act).astype(jnp.bfloat16)


def shards(
    tokens,
    norm_gain,
    w_query,
    w_key,
    w_value,
    w_gate,
    w_beta,
    w_decay,
    conv_query,
    conv_key,
    conv_value,
    decay_rate,
    dt_bias,
    out_gain,
    seg_ids,
):
    gathered = (
        lax.all_gather(w_query, "dp", axis=0, tiled=True),
        lax.all_gather(w_key, "dp", axis=0, tiled=True),
        lax.all_gather(w_value, "dp", axis=0, tiled=True),
        lax.all_gather(w_gate, "dp", axis=0, tiled=True),
        lax.all_gather(w_beta, "dp", axis=0, tiled=True),
        lax.all_gather(w_decay, "dp", axis=0, tiled=True),
    )
    column_counts = [matrix.shape[1] for matrix in gathered]
    joined = jnp.concatenate(gathered, axis=1)
    projected = jnp.dot(
        rms_rows(lax.all_gather(tokens, "tp", axis=0, tiled=True), norm_gain),
        joined,
        preferred_element_type=jnp.float32,
    ).astype(jnp.bfloat16)
    parts = split_columns(projected, column_counts)
    segment = seg_ids[0]
    query, keys, values, beta, log_decay, gate_act = prepare_heads(
        parts, segment, conv_query, conv_key, conv_value, decay_rate, dt_bias
    )
    row_count = values.shape[0]
    local_heads = values.shape[1]
    mixed = jax.vmap(delta_head, in_axes=(1, 1, 1, 1, 1, None), out_axes=1)(
        query, keys, values, beta, log_decay, segment
    )
    tiles = finish_heads(mixed, gate_act, out_gain).reshape(row_count, local_heads * DV)
    return lax.all_to_all(tiles, "tp", split_axis=0, concat_axis=1, tiled=True)


MESH = pl.DeviceIdType.MESH
CORES = 2
STEP = 8


def dot_exact(left, right):
    return jnp.dot(left, right, precision=highest, preferred_element_type=jnp.float32)


def dot_rows(left, right, precision=None):
    return lax.dot_general(
        left,
        right,
        (((1,), (1,)), ((), ())),
        precision=precision,
        preferred_element_type=jnp.float32,
    )


def sigmoid(x):
    return 1.0 / (1.0 + jnp.exp(-x))


def unit_rows(values):
    return values * lax.rsqrt(jnp.sum(values * values, axis=-1, keepdims=True) + 1e-06)


def conv_rows(projected, taps, same_before):
    summed = projected * taps[3:4]
    for offset in range(1, 4):
        shifted = pltpu.roll(projected, offset, 0)
        mask = same_before[offset - 1]
        if projected.shape[1] > mask.shape[1]:
            mask = jnp.concatenate([mask] * (projected.shape[1] // mask.shape[1]), axis=1)
        summed = summed + jnp.where(mask, shifted, 0.0) * taps[3 - offset : 4 - offset]
    return summed * sigmoid(summed)


def inverse_blocks(lows, row, col, rows):
    eye = jnp.where(row == col, 1.0, 0.0)

    def block(size):
        return row // size == col // size

    inner = [jnp.where(block(STEP), m, 0.0) for m in lows]
    squares = [dot_exact(m, m) for m in inner]
    fourths = [dot_exact(m, m) for m in squares]
    firsts = [eye - m + s - dot_exact(m, s) for m, s in zip(inner, squares)]
    inverse = [f + dot_exact(f, q) for f, q in zip(firsts, fourths)]
    size = STEP
    while size < rows // 4:
        ring = block(2 * size) & jnp.logical_not(block(size))
        parts = [dot_exact(jnp.where(ring, m, 0.0), t) for m, t in zip(lows, inverse)]
        inverse = [t - dot_exact(t, p) for t, p in zip(inverse, parts)]
        size = 2 * size
    outer = jnp.logical_not(block(size))
    return inverse, [jnp.where(outer, m, 0.0) for m in lows]


def layer_kernel(
    nz,
    ntp,
    heads,
    tokens_hbm,
    gain_hbm,
    w_query,
    w_key,
    w_value,
    w_gate,
    beta_hbm,
    decay_hbm,
    taps_q_hbm,
    taps_k_hbm,
    taps_v_hbm,
    rate_hbm,
    bias_hbm,
    out_gain_hbm,
    seg_hbm,
    out,
    tokens,
    norm_gain,
    w_beta,
    w_decay,
    taps_q,
    taps_k,
    taps_v,
    rate,
    bias,
    out_gain,
    tok,
    w_first,
    w_second,
    w_third,
    ba,
    seg,
    tiles,
    loads,
    zs,
    zr,
    fs,
    fr,
    ys,
    yr,
    ws,
    wr,
    os,
    orr,
    rs,
    rr,
    bs,
    br,
    brs,
    brr,
    ss,
    sr,
    cs,
    cr,
    local,
):
    dp = lax.axis_index("dp")
    tp = lax.axis_index("tp")
    z = dp // CORES
    core = dp % CORES
    sibling = (z * CORES + 1 - core, tp)
    width = heads * DV

    def z_at(k):
        return lax.rem(z + k, nz)

    def z_from(k):
        return lax.rem(z + nz - k, nz)

    def dp_at(k):
        return z_at(k) * CORES + core

    def tp_at(j):
        return lax.rem(tp + j, ntp)

    def remote(source, target, send, recv, device):
        copy = pltpu.make_async_remote_copy(
            src_ref=source,
            dst_ref=target,
            send_sem=send,
            recv_sem=recv,
            device_id=device,
            device_id_type=MESH,
        )
        copy.start()
        return copy

    def load(i, source, target):
        copy = pltpu.make_async_copy(source, target, loads.at[i])
        copy.start()
        return copy

    early = [
        load(0, tokens_hbm, tokens),
        load(1, gain_hbm, norm_gain),
        load(2, beta_hbm, w_beta),
        load(3, decay_hbm, w_decay),
        load(4, seg_hbm, seg.at[z]),
    ]
    later = [
        load(5, taps_q_hbm, taps_q),
        load(6, taps_k_hbm, taps_k),
        load(7, taps_v_hbm, taps_v),
        load(8, rate_hbm, rate),
        load(9, bias_hbm, bias),
        load(10, out_gain_hbm, out_gain),
    ]

    barrier = pltpu.get_barrier_semaphore()
    for k in range(nz):
        for j in range(ntp):
            if k or j:
                pl.semaphore_signal(
                    barrier, inc=1, device_id=(dp_at(k), tp_at(j)), device_id_type=MESH
                )
    pl.semaphore_signal(barrier, inc=1, device_id=sibling, device_id_type=MESH)

    def columns(chip, size):
        return pl.ds(pl.multiple_of(chip * size, size), size)

    def pieces(chip):
        return (
            (w_query.at[:, columns(chip, DK)], w_first.at[dp, :, 0:DK]),
            (w_key.at[:, columns(chip, DK)], w_first.at[dp, :, DK : 2 * DK]),
            (w_value.at[:, columns(chip, width)], w_second.at[dp]),
            (w_gate.at[:, columns(chip, width)], w_third.at[dp]),
        )

    for copy in early:
        copy.wait()
    own_local = []
    for i, (source, target) in enumerate(pieces(z)):
        copy = pltpu.make_async_copy(source, target, local.at[i])
        copy.start()
        own_local.append(copy)

    floats = tokens[...].astype(jnp.float32)
    scaled = floats * lax.rsqrt(jnp.mean(floats * floats, axis=-1, keepdims=True) + 1e-06)
    tok[z, tp] = (scaled * norm_gain[...]).astype(jnp.bfloat16)
    count = w_beta.shape[1]
    pick_row = lax.broadcasted_iota(jnp.int32, (2 * count, count), 0)
    pick_col = lax.broadcasted_iota(jnp.int32, (2 * count, count), 1)
    pick_beta = jnp.where(pick_row == pick_col, 1.0, 0.0).astype(jnp.bfloat16)
    pick_decay = jnp.where(pick_row == pick_col + count, 1.0, 0.0).astype(jnp.bfloat16)
    ba[dp] = (dot_rows(pick_beta, w_beta[...]) + dot_rows(pick_decay, w_decay[...])).astype(
        jnp.bfloat16
    )

    pl.semaphore_wait(barrier, nz * ntp)

    half = nz // 2
    near = [k for k in range(1, half)]
    far = half
    mirror = z + half - 2 * half * (z // half)

    def in_half(k):
        return (z // half) * half + lax.rem(z + k, half)

    def in_half_from(k):
        return (z // half) * half + lax.rem(z + half - k, half)

    def other(chip):
        return lax.rem(chip + half, nz)

    def device_of(chip):
        return (chip * CORES + core, tp)

    tok_far = remote(
        tok.at[z, tp], tok.at[z, tp], zs.at[far], zr.at[far], device_of(mirror)
    )
    tok_near = [
        remote(tok.at[z, tp], tok.at[z, tp], zs.at[k], zr.at[k], device_of(in_half(k)))
        for k in near
    ]
    seg_z = []
    ba_z = []
    for k in range(1, nz):
        peer = (dp_at(k), tp)
        seg_z.append(remote(seg.at[z], seg.at[z], ss.at[k], sr.at[k], peer))
        ba_z.append(remote(ba.at[dp], ba.at[dp], bs.at[k], br.at[k], peer))

    def spread_rows(n, at):
        return [
            remote(tok.at[at, tp], tok.at[at, tp], ys.at[n, j], yr.at[n, j], (dp, tp_at(j)))
            for j in range(1, ntp)
        ]

    tok_y = spread_rows(0, z)
    farthest = [nz // 2] + [k for k in range(1, nz) if k != nz // 2]
    weight_z = {}
    for i in range(4):
        for k in farthest:
            source, target = pieces(z_at(k))[i]
            weight_z[i, k] = remote(source, target, ws.at[k, i], wr.at[k, i], (dp_at(k), tp))
        if i == 1:
            tok_far.wait_recv()
            tok_pass = [
                remote(
                    tok.at[mirror, tp],
                    tok.at[mirror, tp],
                    fs.at[k],
                    fr.at[k],
                    device_of(in_half(k)),
                )
                for k in near
            ]
            tok_y += spread_rows(1, mirror)
    own_sibling = []
    for i, (source, target) in enumerate(pieces(z)):
        own_sibling.append(remote(source, target, os.at[i], orr.at[i], sibling))
    ba_own = remote(ba.at[dp], ba.at[dp], brs.at[0], brr.at[0], sibling)

    slot = 2
    for k in near:
        tok_near[k - 1].wait_recv()
        tok_y += spread_rows(slot, in_half_from(k))
        tok_pass[k - 1].wait_recv()
        tok_y += spread_rows(slot + 1, other(in_half_from(k)))
        slot += 2

    relays = []

    def relay(stage, which, ref):
        passed = []
        for k in farthest:
            at = z_from(k) * CORES + core
            for i in which:
                weight_z[i, k].wait_recv()
            passed.append(
                remote(ref.at[at], ref.at[at], rs.at[stage, k], rr.at[stage, k], sibling)
            )
        for i in which:
            own_local[i].wait()
            own_sibling[i].wait_recv()
        for copy in passed:
            copy.wait_recv()
        relays.extend(passed)

    for k in range(1, nz):
        at = z_from(k) * CORES + core
        ba_z[k - 1].wait_recv()
        relays.append(remote(ba.at[at], ba.at[at], brs.at[k], brr.at[k], sibling))
    ba_own.wait_recv()
    for copy in list(relays):
        copy.wait_recv()
    for copy in seg_z + tok_y:
        copy.wait_recv()
    for copy in later:
        copy.wait()
    relay(0, (0, 1), w_first)

    rows = seg.shape[2]
    sources, depth = ba.shape[0], ba.shape[2]
    model = tok.shape[3]
    row = lax.broadcasted_iota(jnp.int32, (rows, rows), 0)
    col = lax.broadcasted_iota(jnp.int32, (rows, rows), 1)
    lower = row >= col
    strict = row > col
    ones_lower = jnp.where(lower, 1.0, 0.0)
    lane = lax.broadcasted_iota(jnp.int32, (rows, count), 1)

    def project(chip, ref):
        left = tok[chip].reshape(rows, model)
        right = ref[...].reshape(sources * depth, ref.shape[2])
        result = jnp.dot(left, right, preferred_element_type=jnp.float32)
        return result.astype(jnp.bfloat16).astype(jnp.float32)

    order = [z_at(k) for k in farthest] + [z]
    tq = taps_q[:, columns(z, DK)]
    tk = taps_k[:, columns(z, DK)]
    tv = taps_v[:, columns(z, width)]
    lows, scores, betas, befores = [], [], [], []
    for chip in order:
        projected = project(chip, w_first)
        left = tok[chip].reshape(rows, model)
        small = jnp.zeros((rows, 2 * count), jnp.float32)
        for s in range(sources):
            small = small + dot_rows(left[:, s * depth : (s + 1) * depth], ba[s])
        small = small.astype(jnp.bfloat16).astype(jnp.float32)
        beta_all = sigmoid(small[:, :count])
        shifted = small[:, count:] + bias[...]
        soft = jnp.maximum(shifted, 0.0) + jnp.log1p(jnp.exp(-jnp.abs(shifted)))
        cumulative = dot_exact(ones_lower, -rate[...] * soft)
        seg_row = jnp.broadcast_to(seg[chip].astype(jnp.float32), (rows, rows))
        seg_col = seg_row.T
        same = seg_row == seg_col
        same_before = [
            (pltpu.roll(seg_col, offset, 0) == seg_col) & (row >= offset) for offset in range(1, 4)
        ]
        query = unit_rows(conv_rows(projected[:, :DK], tq, same_before)) * DK ** (-0.5)
        key = unit_rows(conv_rows(projected[:, DK:], tk, same_before))
        key_gram = dot_rows(key, key, highest)
        query_gram = dot_rows(query, key, highest)
        befores.append(same_before)
        for h in range(heads):
            pick = lane == z * heads + h
            beta = jnp.sum(jnp.where(pick, beta_all, 0.0), axis=1, keepdims=True)
            total = jnp.sum(jnp.where(pick, cumulative, 0.0), axis=1, keepdims=True)
            total = jnp.broadcast_to(total, (rows, rows))
            spread = jnp.where(lower, total - total.T, 0.0)
            decay = jnp.where(lower & same, jnp.exp(spread), 0.0)
            betas.append(beta)
            lows.append(jnp.where(strict, beta * key_gram * decay, 0.0))
            scores.append(query_gram * decay)
    inverse, outer = inverse_blocks(lows, row, col, rows)

    relay(1, (2,), w_second)
    rights = []
    for n, chip in enumerate(order):
        values = conv_rows(project(chip, w_second), tv, befores[n])
        for h in range(heads):
            rights.append(betas[n * heads + h] * values[:, h * DV : (h + 1) * DV])
    solved = [dot_exact(t, b) for t, b in zip(inverse, rights)]
    parts = [dot_exact(m, x) for m, x in zip(outer, solved)]
    solved = [x - dot_exact(t, p) for x, t, p in zip(solved, inverse, parts)]
    mixed = [dot_exact(s, x) for s, x in zip(scores, solved)]
    normed = [
        m * lax.rsqrt(jnp.mean(m * m, axis=-1, keepdims=True) + 1e-06) * out_gain[...]
        for m in mixed
    ]

    relay(2, (3,), w_third)
    place = columns(tp * nz + z, width)
    share = rows // ntp
    finals = []
    for n, chip in enumerate(order):
        gate = project(chip, w_third)
        gate = gate * sigmoid(gate)
        both = jnp.concatenate(normed[n * heads : (n + 1) * heads], axis=1)
        tile = (both * gate).astype(jnp.bfloat16)
        for t in range(ntp):
            tiles[chip, t] = tile[t * share : (t + 1) * share]
        k = (farthest + [0])[n]
        for j in range(ntp):
            source = tiles.at[chip, tp_at(j)]
            if k or j:
                finals.append(
                    remote(
                        source, out.at[:, place], cs.at[k, j], cr.at[k, j], (dp_at(k), tp_at(j))
                    )
                )
            else:
                copy = pltpu.make_async_copy(source, out.at[:, place], cs.at[0, 0])
                copy.start()
                finals.append(copy)
    for copy in [tok_far] + tok_near + tok_pass + seg_z + tok_y + ba_z + [ba_own]:
        copy.wait_send()
    for copy in list(weight_z.values()) + own_sibling + relays:
        copy.wait_send()
    for copy in finals:
        copy.wait()


def layer(n_dp, n_tp, *args):
    (
        tokens,
        norm_gain,
        w_query,
        w_key,
        w_value,
        w_gate,
        w_beta,
        w_decay,
        conv_query,
        conv_key,
        conv_value,
        decay_rate,
        dt_bias,
        out_gain,
        seg_ids,
    ) = args
    nz = n_dp // CORES
    rows = seg_ids.shape[1]
    share, model = tokens.shape
    depth = w_query.shape[0]
    value_heads = w_value.shape[1] // DV
    if n_dp % (2 * CORES) or w_query.shape[1] // DK != nz or value_heads % nz or rows != 128:
        return shards(*args)
    heads = value_heads // nz
    small = 2 * value_heads
    hbm = pl.BlockSpec(memory_space=pltpu.HBM)
    dma = pltpu.SemaphoreType.DMA
    one_row = norm_gain.reshape(1, -1), decay_rate.reshape(1, -1), dt_bias.reshape(1, -1)
    gain = out_gain.reshape(1, -1)
    held = (tokens, one_row[0], w_beta, w_decay, conv_query, conv_key, conv_value)
    held += one_row[1:] + (gain,)
    return pl.pallas_call(
        functools.partial(layer_kernel, nz, n_tp, heads),
        out_shape=jax.ShapeDtypeStruct((share, n_tp * value_heads * DV), jnp.bfloat16),
        in_specs=[hbm] * 15,
        out_specs=pl.BlockSpec(memory_space=pltpu.VMEM),
        scratch_shapes=[pltpu.VMEM(a.shape, a.dtype) for a in held]
        + [
            pltpu.VMEM((nz, n_tp, share, model), jnp.bfloat16),
            pltpu.VMEM((n_dp, depth, 2 * DK), jnp.bfloat16),
            pltpu.VMEM((n_dp, depth, heads * DV), jnp.bfloat16),
            pltpu.VMEM((n_dp, depth, heads * DV), jnp.bfloat16),
            pltpu.VMEM((n_dp, small, depth), jnp.bfloat16),
            pltpu.VMEM((nz, 1, rows), jnp.int32),
            pltpu.VMEM((nz, n_tp, share, heads * DV), jnp.bfloat16),
            dma((11,)),
            dma((nz,)),
            dma((nz,)),
            dma((nz,)),
            dma((nz,)),
            dma((nz, n_tp)),
            dma((nz, n_tp)),
            dma((nz, 4)),
            dma((nz, 4)),
            dma((4,)),
            dma((4,)),
            dma((3, nz)),
            dma((3, nz)),
            dma((nz,)),
            dma((nz,)),
            dma((nz,)),
            dma((nz,)),
            dma((nz,)),
            dma((nz,)),
            dma((nz, n_tp)),
            dma((nz, n_tp)),
            dma((4,)),
        ],
        compiler_params=pltpu.CompilerParams(
            collective_id=0, has_side_effects=True, vmem_limit_bytes=60 * 2**20
        ),
    )(
        tokens,
        one_row[0],
        w_query,
        w_key,
        w_value,
        w_gate,
        w_beta,
        w_decay,
        conv_query,
        conv_key,
        conv_value,
        one_row[1],
        one_row[2],
        gain,
        seg_ids,
    )


def solution(mesh):
    in_specs = (
        P(("dp", "tp"), None),
        P(),
        P("dp", "tp"),
        P("dp", "tp"),
        P("dp", "tp"),
        P("dp", "tp"),
        P("dp", "tp"),
        P("dp", "tp"),
        P(None, "tp"),
        P(None, "tp"),
        P(None, "tp"),
        P("tp"),
        P("tp"),
        P(),
        P("dp", None),
    )
    out_specs = P(("dp", "tp"), None)
    body = functools.partial(layer, mesh.shape["dp"], mesh.shape["tp"])
    return jax.shard_map(body, mesh=mesh, in_specs=in_specs, out_specs=out_specs, check_vma=False)
```

```python
import functools

import jax
import jax.numpy as jnp
from jax import lax
from jax.experimental import pallas as pl
from jax.experimental.pallas import tpu as pltpu
from jax.sharding import PartitionSpec as P

DK = 128
DV = 128
SPAN = 64


highest = lax.Precision.HIGHEST


def rms_rows(tokens, gain):
    floats = tokens.astype(jnp.float32)
    scaled = floats * lax.rsqrt(jnp.mean(floats * floats, axis=-1, keepdims=True) + 1e-06)
    return (scaled * gain).astype(jnp.bfloat16)


def split_columns(projected, column_counts):
    pieces = []
    offset = 0
    for count in column_counts:
        pieces.append(projected[:, offset : offset + count])
        offset = offset + count
    return pieces


def causal_conv(projected, kernel, segment):
    kernel_len = kernel.shape[0]
    summed = projected * kernel[kernel_len - 1]
    for offset in range(1, kernel_len):
        zeros_top = jnp.zeros((offset, projected.shape[1]), jnp.float32)
        shifted = jnp.concatenate([zeros_top, projected[:-offset]], axis=0)
        earlier = jnp.concatenate([jnp.full((offset,), -1, jnp.int32), segment[:-offset]])
        same_doc = (earlier == segment).astype(jnp.float32)
        summed = summed + shifted * same_doc[:, None] * kernel[kernel_len - 1 - offset]
    return jax.nn.silu(summed)


def unit_heads(values, heads, head_size):
    shaped = values.reshape(values.shape[0], heads, head_size)
    return shaped * lax.rsqrt(jnp.sum(shaped * shaped, axis=-1, keepdims=True) + 1e-06)


def delta_head(query, key_rows, value, beta, log_decay, segment):
    row_count = query.shape[0]
    blocks = row_count // SPAN
    value_size = value.shape[1]
    q_blocks = query.reshape(blocks, SPAN, query.shape[1])
    k_blocks = key_rows.reshape(blocks, SPAN, key_rows.shape[1])
    v_blocks = value.reshape(blocks, SPAN, value_size)
    beta_blocks = beta.reshape(blocks, SPAN)
    decay_blocks = log_decay.reshape(blocks, SPAN)
    seg_blocks = segment.reshape(blocks, SPAN)
    before = jnp.concatenate([jnp.full((1,), -1, jnp.int32), seg_blocks[:-1, -1]])
    row_index = lax.broadcasted_iota(jnp.int32, (SPAN, SPAN), 0)
    col_index = lax.broadcasted_iota(jnp.int32, (SPAN, SPAN), 1)
    lower_mask = row_index >= col_index
    strict = row_index > col_index

    def advance(state, inputs):
        block_q, block_k, block_v, block_beta, block_decay, block_seg, block_before = inputs
        cumulative = jnp.cumsum(block_decay)
        same_doc = block_seg[:, None] == block_seg[None, :]
        spread = jnp.where(lower_mask, cumulative[:, None] - cumulative[None, :], 0.0)
        decay_matrix = jnp.where(lower_mask & same_doc, jnp.exp(spread), 0.0)
        carried = (block_seg == block_before).astype(jnp.float32)
        from_start = jnp.exp(cumulative) * carried
        key_gram = jnp.dot(block_k, block_k.T, precision=highest)
        lower_matrix = jnp.where(strict, block_beta[:, None] * key_gram * decay_matrix, 0.0)
        system = jnp.eye(SPAN, dtype=jnp.float32) + lower_matrix
        right_side = jnp.concatenate(
            [block_beta[:, None] * block_v, (block_beta * from_start)[:, None] * block_k], axis=1
        )
        solved = lax.linalg.triangular_solve(
            system, right_side, left_side=True, lower=True, unit_diagonal=True
        )
        updates = solved[:, :value_size] - jnp.dot(solved[:, value_size:], state, precision=highest)
        scores = jnp.dot(block_q, block_k.T, precision=highest) * decay_matrix
        output = jnp.dot(from_start[:, None] * block_q, state, precision=highest) + jnp.dot(
            scores, updates, precision=highest
        )
        tail_weight = jnp.where(
            block_seg == block_seg[-1], jnp.exp(cumulative[-1] - cumulative), 0.0
        )
        new_state = jnp.exp(cumulative[-1]) * carried[-1] * state + jnp.dot(
            (tail_weight[:, None] * block_k).T, updates, precision=highest
        )
        return (new_state, output)

    initial = jnp.zeros((key_rows.shape[1], value_size), jnp.float32)
    last_state, outputs = lax.scan(
        advance,
        initial,
        (q_blocks, k_blocks, v_blocks, beta_blocks, decay_blocks, seg_blocks, before),
    )
    return outputs.reshape(row_count, value_size)


def prepare_heads(parts, segment, conv_query, conv_key, conv_value, decay_rate, dt_bias):
    proj_query, proj_key, proj_value, proj_gate, proj_beta, proj_decay = [
        piece_part.astype(jnp.float32) for piece_part in parts
    ]
    key_heads = proj_query.shape[1] // DK
    value_heads = proj_value.shape[1] // DV
    repeat = value_heads // key_heads
    query = unit_heads(causal_conv(proj_query, conv_query, segment), key_heads, DK) * DK ** (-0.5)
    keys = unit_heads(causal_conv(proj_key, conv_key, segment), key_heads, DK)
    values = causal_conv(proj_value, conv_value, segment).reshape(
        proj_value.shape[0], value_heads, DV
    )
    query = jnp.repeat(query, repeat, axis=1)
    keys = jnp.repeat(keys, repeat, axis=1)
    beta = jax.nn.sigmoid(proj_beta)
    log_decay = -decay_rate * jax.nn.softplus(proj_decay + dt_bias)
    gate_act = jax.nn.silu(proj_gate.reshape(proj_gate.shape[0], value_heads, DV))
    return (query, keys, values, beta, log_decay, gate_act)


def finish_heads(mixed, gate_act, out_gain):
    normed = mixed * lax.rsqrt(jnp.mean(mixed * mixed, axis=-1, keepdims=True) + 1e-06) * out_gain
    return (normed * gate_act).astype(jnp.bfloat16)


def shards(
    tokens,
    norm_gain,
    w_query,
    w_key,
    w_value,
    w_gate,
    w_beta,
    w_decay,
    conv_query,
    conv_key,
    conv_value,
    decay_rate,
    dt_bias,
    out_gain,
    seg_ids,
):
    gathered = (
        lax.all_gather(w_query, "dp", axis=0, tiled=True),
        lax.all_gather(w_key, "dp", axis=0, tiled=True),
        lax.all_gather(w_value, "dp", axis=0, tiled=True),
        lax.all_gather(w_gate, "dp", axis=0, tiled=True),
        lax.all_gather(w_beta, "dp", axis=0, tiled=True),
        lax.all_gather(w_decay, "dp", axis=0, tiled=True),
    )
    column_counts = [matrix.shape[1] for matrix in gathered]
    joined = jnp.concatenate(gathered, axis=1)
    projected = jnp.dot(
        rms_rows(lax.all_gather(tokens, "tp", axis=0, tiled=True), norm_gain),
        joined,
        preferred_element_type=jnp.float32,
    ).astype(jnp.bfloat16)
    parts = split_columns(projected, column_counts)
    segment = seg_ids[0]
    query, keys, values, beta, log_decay, gate_act = prepare_heads(
        parts, segment, conv_query, conv_key, conv_value, decay_rate, dt_bias
    )
    row_count = values.shape[0]
    local_heads = values.shape[1]
    mixed = jax.vmap(delta_head, in_axes=(1, 1, 1, 1, 1, None), out_axes=1)(
        query, keys, values, beta, log_decay, segment
    )
    tiles = finish_heads(mixed, gate_act, out_gain).reshape(row_count, local_heads * DV)
    return lax.all_to_all(tiles, "tp", split_axis=0, concat_axis=1, tiled=True)


MESH = pl.DeviceIdType.MESH
CORES = 2
STEP = 8


def dot_exact(left, right):
    return jnp.dot(left, right, precision=highest, preferred_element_type=jnp.float32)


def dot_rows(left, right, precision=None):
    return lax.dot_general(
        left,
        right,
        (((1,), (1,)), ((), ())),
        precision=precision,
        preferred_element_type=jnp.float32,
    )


def two_parts(values):
    high = values.astype(jnp.bfloat16)
    low = (values - high.astype(jnp.float32)).astype(jnp.bfloat16)
    return high, low


def product(left, right):
    left_parts = jnp.concatenate(two_parts(left), axis=1)
    right_parts = jnp.concatenate(two_parts(right), axis=1)
    right_parts = jnp.concatenate([right_parts, right_parts], axis=0)
    both = jnp.dot(left_parts, right_parts, preferred_element_type=jnp.float32)
    size = right.shape[1]
    return both[:, :size] + both[:, size:]


def product_rows(left, right):
    left_parts = jnp.concatenate(two_parts(left), axis=1)
    right_parts = jnp.concatenate(two_parts(right), axis=0)
    right_parts = jnp.concatenate([right_parts, right_parts], axis=1)
    both = dot_rows(left_parts, right_parts)
    size = right.shape[0]
    return both[:, :size] + both[:, size:]


def sigmoid(x):
    return 1.0 / (1.0 + jnp.exp(-x))


def unit_rows(values):
    return values * lax.rsqrt(jnp.sum(values * values, axis=-1, keepdims=True) + 1e-06)


def conv_rows(projected, taps, same_before):
    summed = projected * taps[3:4]
    for offset in range(1, 4):
        shifted = pltpu.roll(projected, offset, 0)
        mask = same_before[offset - 1]
        if projected.shape[1] > mask.shape[1]:
            mask = jnp.concatenate([mask] * (projected.shape[1] // mask.shape[1]), axis=1)
        summed = summed + jnp.where(mask, shifted, 0.0) * taps[3 - offset : 4 - offset]
    return summed * sigmoid(summed)


def inverse_blocks(lows, row, col, rows):
    eye = jnp.where(row == col, 1.0, 0.0)

    def block(size):
        return row // size == col // size

    inner = [jnp.where(block(STEP), m, 0.0) for m in lows]
    squares = [product(m, m) for m in inner]
    fourths = [product(m, m) for m in squares]
    firsts = [eye - m + s - product(m, s) for m, s in zip(inner, squares)]
    inverse = [f + product(f, q) for f, q in zip(firsts, fourths)]
    size = STEP
    while size < rows // 4:
        ring = block(2 * size) & jnp.logical_not(block(size))
        parts = [product(jnp.where(ring, m, 0.0), t) for m, t in zip(lows, inverse)]
        inverse = [t - product(t, p) for t, p in zip(inverse, parts)]
        size = 2 * size
    outer = jnp.logical_not(block(size))
    return inverse, [jnp.where(outer, m, 0.0) for m in lows]


def layer_kernel(
    nz,
    ntp,
    heads,
    tokens_hbm,
    gain_hbm,
    w_query,
    w_key,
    w_value,
    w_gate,
    beta_hbm,
    decay_hbm,
    taps_q_hbm,
    taps_k_hbm,
    taps_v_hbm,
    rate_hbm,
    bias_hbm,
    out_gain_hbm,
    seg_hbm,
    out,
    tokens,
    norm_gain,
    w_beta,
    w_decay,
    taps_q,
    taps_k,
    taps_v,
    rate,
    bias,
    out_gain,
    tok,
    w_first,
    w_second,
    w_third,
    ba,
    seg,
    tiles,
    loads,
    zs,
    zr,
    ys,
    yr,
    ws,
    wr,
    os,
    orr,
    rs,
    rr,
    bs,
    br,
    brs,
    brr,
    ss,
    sr,
    cs,
    cr,
    local,
):
    dp = lax.axis_index("dp")
    tp = lax.axis_index("tp")
    z = dp // CORES
    core = dp % CORES
    sibling = (z * CORES + 1 - core, tp)
    width = heads * DV

    def z_at(k):
        return lax.rem(z + k, nz)

    def dp_at(k):
        return z_at(k) * CORES + core

    def tp_at(j):
        return lax.rem(tp + j, ntp)

    def remote(source, target, send, recv, device):
        copy = pltpu.make_async_remote_copy(
            src_ref=source,
            dst_ref=target,
            send_sem=send,
            recv_sem=recv,
            device_id=device,
            device_id_type=MESH,
        )
        copy.start()
        return copy

    def load(i, source, target):
        copy = pltpu.make_async_copy(source, target, loads.at[i])
        copy.start()
        return copy

    early = [
        load(0, tokens_hbm, tokens),
        load(1, gain_hbm, norm_gain),
        load(2, beta_hbm, w_beta),
        load(3, decay_hbm, w_decay),
        load(4, seg_hbm, seg.at[0]),
    ]
    later = [
        load(5, taps_q_hbm, taps_q),
        load(6, taps_k_hbm, taps_k),
        load(7, taps_v_hbm, taps_v),
        load(8, rate_hbm, rate),
        load(9, bias_hbm, bias),
        load(10, out_gain_hbm, out_gain),
    ]

    barrier = pltpu.get_barrier_semaphore()
    for k in range(nz):
        for j in range(ntp):
            if k or j:
                pl.semaphore_signal(
                    barrier, inc=1, device_id=(dp_at(k), tp_at(j)), device_id_type=MESH
                )
    pl.semaphore_signal(barrier, inc=1, device_id=sibling, device_id_type=MESH)

    def columns(chip, size):
        return pl.ds(pl.multiple_of(chip * size, size), size)

    def pieces(chip):
        return (
            (w_query.at[:, columns(chip, DK)], w_first.at[dp, :, 0:DK]),
            (w_key.at[:, columns(chip, DK)], w_first.at[dp, :, DK : 2 * DK]),
            (w_value.at[:, columns(chip, width)], w_second.at[dp]),
        ) + tuple(
            (w_gate.at[:, columns(chip * heads + h, DV)], w_third.at[h, dp]) for h in range(heads)
        )

    for copy in early:
        copy.wait()
    own_local = []
    for i, (source, target) in enumerate(pieces(z)):
        copy = pltpu.make_async_copy(source, target, local.at[i])
        copy.start()
        own_local.append(copy)

    floats = tokens[...].astype(jnp.float32)
    scaled = floats * lax.rsqrt(jnp.mean(floats * floats, axis=-1, keepdims=True) + 1e-06)
    tok[0, tp] = (scaled * norm_gain[...]).astype(jnp.bfloat16)
    count = w_beta.shape[0]
    narrow = [w_beta[...].astype(jnp.float32), w_decay[...].astype(jnp.float32)]
    ba[dp] = jnp.concatenate(narrow, axis=0).astype(jnp.bfloat16)

    pl.semaphore_wait(barrier, nz * ntp)

    half = nz // 2
    base = (z // half) * half
    mirror = lax.rem(z + half, nz)
    targets = [z, mirror]
    sources = [z, mirror]
    for k in range(1, half):
        ahead = base + lax.rem(z + k, half)
        behind = base + lax.rem(z + half - k, half)
        targets += [ahead, lax.rem(ahead + half, nz)]
        sources += [behind, lax.rem(behind + half, nz)]
    others = range(1, nz)
    evens = range(2, nz, 2)

    def device_of(chip):
        return (chip * CORES + core, tp)

    def send_rows(source, slot):
        return remote(
            tok.at[source, tp],
            tok.at[slot, tp],
            zs.at[slot],
            zr.at[slot],
            device_of(targets[slot - source]),
        )

    def spread_rows(slot):
        return [
            remote(
                tok.at[slot, tp], tok.at[slot, tp], ys.at[slot, j], yr.at[slot, j], (dp, tp_at(j))
            )
            for j in range(1, ntp)
        ]

    tok_z = {1: send_rows(0, 1)}
    for n in evens:
        tok_z[n] = send_rows(0, n)
    tok_y = {0: spread_rows(0)}
    seg_z = []
    ba_z = []
    for n in others:
        peer = device_of(targets[n])
        seg_z.append(remote(seg.at[0], seg.at[n], ss.at[n], sr.at[n], peer))
        ba_z.append(remote(ba.at[dp], ba.at[dp], bs.at[n], br.at[n], peer))

    weight_z = {}
    for i in range(3 + heads):
        for n in others:
            source, target = pieces(targets[n])[i]
            weight_z[i, n] = remote(
                source, target, ws.at[n, i], wr.at[n, i], device_of(targets[n])
            )
        if i == 1:
            tok_z[1].wait_recv()
            for n in evens:
                tok_z[n + 1] = send_rows(1, n + 1)
            tok_y[1] = spread_rows(1)
    own_sibling = []
    for i, (source, target) in enumerate(pieces(z)):
        own_sibling.append(remote(source, target, os.at[i], orr.at[i], sibling))
    ba_own = remote(ba.at[dp], ba.at[dp], brs.at[0], brr.at[0], sibling)
    for n in range(2, nz):
        tok_z[n].wait_recv()
        tok_y[n] = spread_rows(n)

    relays = []

    def relay(stage, which, ref):
        passed = []
        for n in others:
            at = sources[n] * CORES + core
            for i in which:
                weight_z[i, n].wait_recv()
            passed.append(
                remote(ref.at[at], ref.at[at], rs.at[stage, n], rr.at[stage, n], sibling)
            )
        for i in which:
            own_local[i].wait()
            own_sibling[i].wait_recv()
        for copy in passed:
            copy.wait_recv()
        relays.extend(passed)

    for n in others:
        at = sources[n] * CORES + core
        ba_z[n - 1].wait_recv()
        relays.append(remote(ba.at[at], ba.at[at], brs.at[n], brr.at[n], sibling))
    for copy in later:
        copy.wait()
    for copy in [ba_own] + relays + seg_z:
        copy.wait_recv()
    relay(0, (0, 1), w_first)

    rows = seg.shape[2]
    holders, depth = ba.shape[0], ba.shape[2]
    model = tok.shape[3]
    row = lax.broadcasted_iota(jnp.int32, (rows, rows), 0)
    col = lax.broadcasted_iota(jnp.int32, (rows, rows), 1)
    lower = row >= col
    strict = row > col
    ones_lower = jnp.where(lower, 1.0, 0.0)
    lane = lax.broadcasted_iota(jnp.int32, (rows, count), 1)

    def project(first, slots, ref):
        left = tok[first : first + slots].reshape(slots * rows, model)
        right = ref[...].reshape(holders * depth, ref.shape[-1])
        result = jnp.dot(left, right, preferred_element_type=jnp.float32)
        return result.astype(jnp.bfloat16).astype(jnp.float32)

    tq = taps_q[:, columns(z, DK)]
    tk = taps_k[:, columns(z, DK)]
    tv = taps_v[:, columns(z, width)]
    inverse, outer, scores, betas, befores = [], [], [], [], []
    for first in range(0, nz, 2):
        for n in (first, first + 1):
            for copy in tok_y[n]:
                copy.wait_recv()
        pair = project(first, 2, w_first)
        left = tok[first : first + 2].reshape(2 * rows, model)
        small = jnp.zeros((2 * rows, 2 * count), jnp.float32)
        for s in range(holders):
            small = small + dot_rows(left[:, s * depth : (s + 1) * depth], ba[s])
        small = small.astype(jnp.bfloat16).astype(jnp.float32)
        lows = []
        for n in (first, first + 1):
            at = (n - first) * rows
            projected = pair[at : at + rows]
            beta_all = sigmoid(small[at : at + rows, :count])
            shifted = small[at : at + rows, count:] + bias[...]
            soft = jnp.maximum(shifted, 0.0) + jnp.log1p(jnp.exp(-jnp.abs(shifted)))
            cumulative = dot_exact(ones_lower, -rate[...] * soft)
            seg_row = jnp.broadcast_to(seg[n].astype(jnp.float32), (rows, rows))
            seg_col = seg_row.T
            same = seg_row == seg_col
            same_before = [
                (pltpu.roll(seg_col, offset, 0) == seg_col) & (row >= offset)
                for offset in range(1, 4)
            ]
            query = unit_rows(conv_rows(projected[:, :DK], tq, same_before)) * DK ** (-0.5)
            key = unit_rows(conv_rows(projected[:, DK:], tk, same_before))
            key_gram = product_rows(key, key)
            query_gram = product_rows(query, key)
            befores.append(same_before)
            for h in range(heads):
                pick = lane == z * heads + h
                beta = jnp.sum(jnp.where(pick, beta_all, 0.0), axis=1, keepdims=True)
                total = jnp.sum(jnp.where(pick, cumulative, 0.0), axis=1, keepdims=True)
                total = jnp.broadcast_to(total, (rows, rows))
                spread = jnp.where(lower, total - total.T, 0.0)
                decay = jnp.where(lower & same, jnp.exp(spread), 0.0)
                betas.append(beta)
                lows.append(jnp.where(strict, beta * key_gram * decay, 0.0))
                scores.append(query_gram * decay)
        blocks, rest = inverse_blocks(lows, row, col, rows)
        inverse += blocks
        outer += rest

    relay(1, (2,), w_second)
    rights = []
    projected = project(0, nz, w_second)
    for n in range(nz):
        values = conv_rows(projected[n * rows : (n + 1) * rows], tv, befores[n])
        for h in range(heads):
            rights.append(betas[n * heads + h] * values[:, h * DV : (h + 1) * DV])
    solved = [product(t, b) for t, b in zip(inverse, rights)]
    parts = [product(m, x) for m, x in zip(outer, solved)]
    solved = [x - product(t, p) for x, t, p in zip(solved, inverse, parts)]
    mixed = [product(s, x) for s, x in zip(scores, solved)]
    normed = [
        m * lax.rsqrt(jnp.mean(m * m, axis=-1, keepdims=True) + 1e-06) * out_gain[...]
        for m in mixed
    ]

    share = rows // ntp
    finals = []
    for h in range(heads):
        relay(2 + h, (3 + h,), w_third.at[h])
        place = columns((tp * nz + z) * heads + h, DV)
        gates = project(0, nz, w_third.at[h])
        for n in list(others) + [0]:
            gate = gates[n * rows : (n + 1) * rows]
            tile = (normed[n * heads + h] * (gate * sigmoid(gate))).astype(jnp.bfloat16)
            for t in range(ntp):
                tiles[h, n, t] = tile[t * share : (t + 1) * share]
            for j in range(ntp):
                source = tiles.at[h, n, tp_at(j)]
                target = out.at[:, place]
                if n or j:
                    device = (sources[n] * CORES + core, tp_at(j))
                    finals.append(remote(source, target, cs.at[h, n, j], cr.at[h, n, j], device))
                else:
                    copy = pltpu.make_async_copy(source, target, cs.at[h, 0, 0])
                    copy.start()
                    finals.append(copy)
    for copy in list(tok_z.values()) + sum(tok_y.values(), []) + seg_z + ba_z + [ba_own]:
        copy.wait_send()
    for copy in list(weight_z.values()) + own_sibling + relays:
        copy.wait_send()
    for copy in finals:
        copy.wait()


def layer(n_dp, n_tp, *args):
    (
        tokens,
        norm_gain,
        w_query,
        w_key,
        w_value,
        w_gate,
        w_beta,
        w_decay,
        conv_query,
        conv_key,
        conv_value,
        decay_rate,
        dt_bias,
        out_gain,
        seg_ids,
    ) = args
    nz = n_dp // CORES
    rows = seg_ids.shape[1]
    share, model = tokens.shape
    depth = w_query.shape[0]
    value_heads = w_value.shape[1] // DV
    if n_dp % (2 * CORES) or w_query.shape[1] // DK != nz or value_heads % nz or rows != 128:
        return shards(*args)
    heads = value_heads // nz
    small = 2 * value_heads
    hbm = pl.BlockSpec(memory_space=pltpu.HBM)
    dma = pltpu.SemaphoreType.DMA
    one_row = norm_gain.reshape(1, -1), decay_rate.reshape(1, -1), dt_bias.reshape(1, -1)
    gain = out_gain.reshape(1, -1)
    narrow = w_beta.T, w_decay.T
    held = (tokens, one_row[0], *narrow, conv_query, conv_key, conv_value)
    held += one_row[1:] + (gain,)
    return pl.pallas_call(
        functools.partial(layer_kernel, nz, n_tp, heads),
        out_shape=jax.ShapeDtypeStruct((share, n_tp * value_heads * DV), jnp.bfloat16),
        in_specs=[hbm] * 15,
        out_specs=hbm,
        scratch_shapes=[pltpu.VMEM(a.shape, a.dtype) for a in held]
        + [
            pltpu.VMEM((nz, n_tp, share, model), jnp.bfloat16),
            pltpu.VMEM((n_dp, depth, 2 * DK), jnp.bfloat16),
            pltpu.VMEM((n_dp, depth, heads * DV), jnp.bfloat16),
            pltpu.VMEM((heads, n_dp, depth, DV), jnp.bfloat16),
            pltpu.VMEM((n_dp, small, depth), jnp.bfloat16),
            pltpu.VMEM((nz, 1, rows), jnp.int32),
            pltpu.VMEM((heads, nz, n_tp, share, DV), jnp.bfloat16),
            dma((11,)),
            dma((nz,)),
            dma((nz,)),
            dma((nz, n_tp)),
            dma((nz, n_tp)),
            dma((nz, 3 + heads)),
            dma((nz, 3 + heads)),
            dma((3 + heads,)),
            dma((3 + heads,)),
            dma((2 + heads, nz)),
            dma((2 + heads, nz)),
            dma((nz,)),
            dma((nz,)),
            dma((nz,)),
            dma((nz,)),
            dma((nz,)),
            dma((nz,)),
            dma((heads, nz, n_tp)),
            dma((heads, nz, n_tp)),
            dma((3 + heads,)),
        ],
        compiler_params=pltpu.CompilerParams(
            collective_id=0, has_side_effects=True, vmem_limit_bytes=60 * 2**20
        ),
    )(
        tokens,
        one_row[0],
        w_query,
        w_key,
        w_value,
        w_gate,
        *narrow,
        conv_query,
        conv_key,
        conv_value,
        one_row[1],
        one_row[2],
        gain,
        seg_ids,
    )


def solution(mesh):
    in_specs = (
        P(("dp", "tp"), None),
        P(),
        P("dp", "tp"),
        P("dp", "tp"),
        P("dp", "tp"),
        P("dp", "tp"),
        P("dp", "tp"),
        P("dp", "tp"),
        P(None, "tp"),
        P(None, "tp"),
        P(None, "tp"),
        P("tp"),
        P("tp"),
        P(),
        P("dp", None),
    )
    out_specs = P(("dp", "tp"), None)
    body = functools.partial(layer, mesh.shape["dp"], mesh.shape["tp"])
    return jax.shard_map(body, mesh=mesh, in_specs=in_specs, out_specs=out_specs, check_vma=False)
```

```python
import functools

import jax
import jax.numpy as jnp
from jax import lax
from jax.experimental import pallas as pl
from jax.experimental.pallas import tpu as pltpu
from jax.sharding import PartitionSpec as P

DK = 128
DV = 128
SPAN = 64


highest = lax.Precision.HIGHEST


def rms_rows(tokens, gain):
    floats = tokens.astype(jnp.float32)
    scaled = floats * lax.rsqrt(jnp.mean(floats * floats, axis=-1, keepdims=True) + 1e-06)
    return (scaled * gain).astype(jnp.bfloat16)


def split_columns(projected, column_counts):
    pieces = []
    offset = 0
    for count in column_counts:
        pieces.append(projected[:, offset : offset + count])
        offset = offset + count
    return pieces


def causal_conv(projected, kernel, segment):
    kernel_len = kernel.shape[0]
    summed = projected * kernel[kernel_len - 1]
    for offset in range(1, kernel_len):
        zeros_top = jnp.zeros((offset, projected.shape[1]), jnp.float32)
        shifted = jnp.concatenate([zeros_top, projected[:-offset]], axis=0)
        earlier = jnp.concatenate([jnp.full((offset,), -1, jnp.int32), segment[:-offset]])
        same_doc = (earlier == segment).astype(jnp.float32)
        summed = summed + shifted * same_doc[:, None] * kernel[kernel_len - 1 - offset]
    return jax.nn.silu(summed)


def unit_heads(values, heads, head_size):
    shaped = values.reshape(values.shape[0], heads, head_size)
    return shaped * lax.rsqrt(jnp.sum(shaped * shaped, axis=-1, keepdims=True) + 1e-06)


def delta_head(query, key_rows, value, beta, log_decay, segment):
    row_count = query.shape[0]
    blocks = row_count // SPAN
    value_size = value.shape[1]
    q_blocks = query.reshape(blocks, SPAN, query.shape[1])
    k_blocks = key_rows.reshape(blocks, SPAN, key_rows.shape[1])
    v_blocks = value.reshape(blocks, SPAN, value_size)
    beta_blocks = beta.reshape(blocks, SPAN)
    decay_blocks = log_decay.reshape(blocks, SPAN)
    seg_blocks = segment.reshape(blocks, SPAN)
    before = jnp.concatenate([jnp.full((1,), -1, jnp.int32), seg_blocks[:-1, -1]])
    row_index = lax.broadcasted_iota(jnp.int32, (SPAN, SPAN), 0)
    col_index = lax.broadcasted_iota(jnp.int32, (SPAN, SPAN), 1)
    lower_mask = row_index >= col_index
    strict = row_index > col_index

    def advance(state, inputs):
        block_q, block_k, block_v, block_beta, block_decay, block_seg, block_before = inputs
        cumulative = jnp.cumsum(block_decay)
        same_doc = block_seg[:, None] == block_seg[None, :]
        spread = jnp.where(lower_mask, cumulative[:, None] - cumulative[None, :], 0.0)
        decay_matrix = jnp.where(lower_mask & same_doc, jnp.exp(spread), 0.0)
        carried = (block_seg == block_before).astype(jnp.float32)
        from_start = jnp.exp(cumulative) * carried
        key_gram = jnp.dot(block_k, block_k.T, precision=highest)
        lower_matrix = jnp.where(strict, block_beta[:, None] * key_gram * decay_matrix, 0.0)
        system = jnp.eye(SPAN, dtype=jnp.float32) + lower_matrix
        right_side = jnp.concatenate(
            [block_beta[:, None] * block_v, (block_beta * from_start)[:, None] * block_k], axis=1
        )
        solved = lax.linalg.triangular_solve(
            system, right_side, left_side=True, lower=True, unit_diagonal=True
        )
        updates = solved[:, :value_size] - jnp.dot(solved[:, value_size:], state, precision=highest)
        scores = jnp.dot(block_q, block_k.T, precision=highest) * decay_matrix
        output = jnp.dot(from_start[:, None] * block_q, state, precision=highest) + jnp.dot(
            scores, updates, precision=highest
        )
        tail_weight = jnp.where(
            block_seg == block_seg[-1], jnp.exp(cumulative[-1] - cumulative), 0.0
        )
        new_state = jnp.exp(cumulative[-1]) * carried[-1] * state + jnp.dot(
            (tail_weight[:, None] * block_k).T, updates, precision=highest
        )
        return (new_state, output)

    initial = jnp.zeros((key_rows.shape[1], value_size), jnp.float32)
    last_state, outputs = lax.scan(
        advance,
        initial,
        (q_blocks, k_blocks, v_blocks, beta_blocks, decay_blocks, seg_blocks, before),
    )
    return outputs.reshape(row_count, value_size)


def prepare_heads(parts, segment, conv_query, conv_key, conv_value, decay_rate, dt_bias):
    proj_query, proj_key, proj_value, proj_gate, proj_beta, proj_decay = [
        piece_part.astype(jnp.float32) for piece_part in parts
    ]
    key_heads = proj_query.shape[1] // DK
    value_heads = proj_value.shape[1] // DV
    repeat = value_heads // key_heads
    query = unit_heads(causal_conv(proj_query, conv_query, segment), key_heads, DK) * DK ** (-0.5)
    keys = unit_heads(causal_conv(proj_key, conv_key, segment), key_heads, DK)
    values = causal_conv(proj_value, conv_value, segment).reshape(
        proj_value.shape[0], value_heads, DV
    )
    query = jnp.repeat(query, repeat, axis=1)
    keys = jnp.repeat(keys, repeat, axis=1)
    beta = jax.nn.sigmoid(proj_beta)
    log_decay = -decay_rate * jax.nn.softplus(proj_decay + dt_bias)
    gate_act = jax.nn.silu(proj_gate.reshape(proj_gate.shape[0], value_heads, DV))
    return (query, keys, values, beta, log_decay, gate_act)


def finish_heads(mixed, gate_act, out_gain):
    normed = mixed * lax.rsqrt(jnp.mean(mixed * mixed, axis=-1, keepdims=True) + 1e-06) * out_gain
    return (normed * gate_act).astype(jnp.bfloat16)


def shards(
    tokens,
    norm_gain,
    w_query,
    w_key,
    w_value,
    w_gate,
    w_beta,
    w_decay,
    conv_query,
    conv_key,
    conv_value,
    decay_rate,
    dt_bias,
    out_gain,
    seg_ids,
):
    gathered = (
        lax.all_gather(w_query, "dp", axis=0, tiled=True),
        lax.all_gather(w_key, "dp", axis=0, tiled=True),
        lax.all_gather(w_value, "dp", axis=0, tiled=True),
        lax.all_gather(w_gate, "dp", axis=0, tiled=True),
        lax.all_gather(w_beta, "dp", axis=0, tiled=True),
        lax.all_gather(w_decay, "dp", axis=0, tiled=True),
    )
    column_counts = [matrix.shape[1] for matrix in gathered]
    joined = jnp.concatenate(gathered, axis=1)
    projected = jnp.dot(
        rms_rows(lax.all_gather(tokens, "tp", axis=0, tiled=True), norm_gain),
        joined,
        preferred_element_type=jnp.float32,
    ).astype(jnp.bfloat16)
    parts = split_columns(projected, column_counts)
    segment = seg_ids[0]
    query, keys, values, beta, log_decay, gate_act = prepare_heads(
        parts, segment, conv_query, conv_key, conv_value, decay_rate, dt_bias
    )
    row_count = values.shape[0]
    local_heads = values.shape[1]
    mixed = jax.vmap(delta_head, in_axes=(1, 1, 1, 1, 1, None), out_axes=1)(
        query, keys, values, beta, log_decay, segment
    )
    tiles = finish_heads(mixed, gate_act, out_gain).reshape(row_count, local_heads * DV)
    return lax.all_to_all(tiles, "tp", split_axis=0, concat_axis=1, tiled=True)


MESH = pl.DeviceIdType.MESH
CORES = 2
STEP = 8


def dot_exact(left, right):
    return jnp.dot(left, right, precision=highest, preferred_element_type=jnp.float32)


def dot_rows(left, right, precision=None):
    return lax.dot_general(
        left,
        right,
        (((1,), (1,)), ((), ())),
        precision=precision,
        preferred_element_type=jnp.float32,
    )


def two_parts(values):
    high = values.astype(jnp.bfloat16)
    low = (values - high.astype(jnp.float32)).astype(jnp.bfloat16)
    return high, low


def product(left, right):
    left_parts = jnp.concatenate(two_parts(left), axis=1)
    right_parts = jnp.concatenate(two_parts(right), axis=1)
    right_parts = jnp.concatenate([right_parts, right_parts], axis=0)
    both = jnp.dot(left_parts, right_parts, preferred_element_type=jnp.float32)
    size = right.shape[1]
    return both[:, :size] + both[:, size:]


def product_rows(left, right):
    left_parts = jnp.concatenate(two_parts(left), axis=1)
    right_parts = jnp.concatenate(two_parts(right), axis=0)
    right_parts = jnp.concatenate([right_parts, right_parts], axis=1)
    both = dot_rows(left_parts, right_parts)
    size = right.shape[0]
    return both[:, :size] + both[:, size:]


def sigmoid(x):
    return 1.0 / (1.0 + jnp.exp(-x))


def unit_rows(values):
    return values * lax.rsqrt(jnp.sum(values * values, axis=-1, keepdims=True) + 1e-06)


def conv_rows(projected, taps, same_before):
    summed = projected * taps[3:4]
    for offset in range(1, 4):
        shifted = pltpu.roll(projected, offset, 0)
        mask = same_before[offset - 1]
        if projected.shape[1] > mask.shape[1]:
            mask = jnp.concatenate([mask] * (projected.shape[1] // mask.shape[1]), axis=1)
        summed = summed + jnp.where(mask, shifted, 0.0) * taps[3 - offset : 4 - offset]
    return summed * sigmoid(summed)


def inverse_blocks(lows, row, col, rows):
    eye = jnp.where(row == col, 1.0, 0.0)

    def block(size):
        return row // size == col // size

    inner = [jnp.where(block(STEP), m, 0.0) for m in lows]
    squares = [product(m, m) for m in inner]
    fourths = [product(m, m) for m in squares]
    firsts = [eye - m + s - product(m, s) for m, s in zip(inner, squares)]
    inverse = [f + product(f, q) for f, q in zip(firsts, fourths)]
    size = STEP
    while size < rows // 4:
        ring = block(2 * size) & jnp.logical_not(block(size))
        parts = [product(jnp.where(ring, m, 0.0), t) for m, t in zip(lows, inverse)]
        inverse = [t - product(t, p) for t, p in zip(inverse, parts)]
        size = 2 * size
    outer = jnp.logical_not(block(size))
    return inverse, [jnp.where(outer, m, 0.0) for m in lows]


def layer_kernel(
    nz,
    ntp,
    heads,
    tokens_hbm,
    gain_hbm,
    w_query,
    w_key,
    w_value,
    w_gate,
    beta_hbm,
    decay_hbm,
    taps_q_hbm,
    taps_k_hbm,
    taps_v_hbm,
    rate_hbm,
    bias_hbm,
    out_gain_hbm,
    seg_hbm,
    out,
    tokens,
    norm_gain,
    w_beta,
    w_decay,
    taps_q,
    taps_k,
    taps_v,
    rate,
    bias,
    out_gain,
    tok,
    w_first,
    w_second,
    w_third,
    ba,
    seg,
    tiles,
    loads,
    zs,
    zr,
    ys,
    yr,
    ws,
    wr,
    os,
    orr,
    rs,
    rr,
    bs,
    br,
    brs,
    brr,
    ss,
    sr,
    cs,
    cr,
    local,
):
    dp = lax.axis_index("dp")
    tp = lax.axis_index("tp")
    z = dp // CORES
    core = dp % CORES
    sibling = (z * CORES + 1 - core, tp)
    width = heads * DV

    def z_at(k):
        return lax.rem(z + k, nz)

    def dp_at(k):
        return z_at(k) * CORES + core

    def tp_at(j):
        return lax.rem(tp + j, ntp)

    def remote(source, target, send, recv, device):
        copy = pltpu.make_async_remote_copy(
            src_ref=source,
            dst_ref=target,
            send_sem=send,
            recv_sem=recv,
            device_id=device,
            device_id_type=MESH,
        )
        copy.start()
        return copy

    def load(i, source, target):
        copy = pltpu.make_async_copy(source, target, loads.at[i])
        copy.start()
        return copy

    early = [
        load(0, tokens_hbm, tokens),
        load(1, gain_hbm, norm_gain),
        load(2, beta_hbm, w_beta),
        load(3, decay_hbm, w_decay),
        load(4, seg_hbm, seg.at[0]),
    ]
    later = [
        load(5, taps_q_hbm, taps_q),
        load(6, taps_k_hbm, taps_k),
        load(7, taps_v_hbm, taps_v),
        load(8, rate_hbm, rate),
        load(9, bias_hbm, bias),
        load(10, out_gain_hbm, out_gain),
    ]

    barrier = pltpu.get_barrier_semaphore()
    for k in range(nz):
        for j in range(ntp):
            if k or j:
                pl.semaphore_signal(
                    barrier, inc=1, device_id=(dp_at(k), tp_at(j)), device_id_type=MESH
                )
    pl.semaphore_signal(barrier, inc=1, device_id=sibling, device_id_type=MESH)

    def columns(chip, size):
        return pl.ds(pl.multiple_of(chip * size, size), size)

    def pieces(chip):
        return (
            (w_query.at[:, columns(chip, DK)], w_first.at[dp, :, 0:DK]),
            (w_key.at[:, columns(chip, DK)], w_first.at[dp, :, DK : 2 * DK]),
            (w_value.at[:, columns(chip, width)], w_second.at[dp]),
        ) + tuple(
            (w_gate.at[:, columns(chip * heads + h, DV)], w_third.at[h, dp]) for h in range(heads)
        )

    for copy in early:
        copy.wait()
    own_local = []
    for i, (source, target) in enumerate(pieces(z)):
        copy = pltpu.make_async_copy(source, target, local.at[i])
        copy.start()
        own_local.append(copy)

    floats = tokens[...].astype(jnp.float32)
    scaled = floats * lax.rsqrt(jnp.mean(floats * floats, axis=-1, keepdims=True) + 1e-06)
    tok[0, tp] = (scaled * norm_gain[...]).astype(jnp.bfloat16)
    count = w_beta.shape[0]
    narrow = [w_beta[...].astype(jnp.float32), w_decay[...].astype(jnp.float32)]
    ba[dp] = jnp.concatenate(narrow, axis=0).astype(jnp.bfloat16)

    pl.semaphore_wait(barrier, nz * ntp)

    half = nz // 2
    base = (z // half) * half
    mirror = lax.rem(z + half, nz)
    targets = [z, mirror]
    sources = [z, mirror]
    for k in range(1, half):
        ahead = base + lax.rem(z + k, half)
        behind = base + lax.rem(z + half - k, half)
        targets += [ahead, lax.rem(ahead + half, nz)]
        sources += [behind, lax.rem(behind + half, nz)]
    others = range(1, nz)
    evens = range(2, nz, 2)
    crossing = list(range(1, nz, 2)) + list(evens)

    def device_of(chip):
        return (chip * CORES + core, tp)

    def send_rows(source, slot):
        return remote(
            tok.at[source, tp],
            tok.at[slot, tp],
            zs.at[slot],
            zr.at[slot],
            device_of(targets[slot - source]),
        )

    def spread_rows(slot):
        return [
            remote(
                tok.at[slot, tp], tok.at[slot, tp], ys.at[slot, j], yr.at[slot, j], (dp, tp_at(j))
            )
            for j in range(1, ntp)
        ]

    tok_z = {1: send_rows(0, 1)}
    for n in evens:
        tok_z[n] = send_rows(0, n)
    tok_y = {0: spread_rows(0)}
    seg_z = []
    ba_z = []
    for n in others:
        peer = device_of(targets[n])
        seg_z.append(remote(seg.at[0], seg.at[n], ss.at[n], sr.at[n], peer))
        ba_z.append(remote(ba.at[dp], ba.at[dp], bs.at[n], br.at[n], peer))

    weight_z = {}

    def send_weights(i):
        for n in crossing:
            source, target = pieces(targets[n])[i]
            weight_z[i, n] = remote(
                source, target, ws.at[n, i], wr.at[n, i], device_of(targets[n])
            )

    send_weights(0)
    send_weights(1)
    tok_z[1].wait_recv()
    for n in evens:
        tok_z[n + 1] = send_rows(1, n + 1)
    tok_y[1] = spread_rows(1)
    own_sibling = []
    for i, (source, target) in enumerate(pieces(z)):
        own_sibling.append(remote(source, target, os.at[i], orr.at[i], sibling))
    ba_own = remote(ba.at[dp], ba.at[dp], brs.at[0], brr.at[0], sibling)
    for n in range(2, nz):
        tok_z[n].wait_recv()
        tok_y[n] = spread_rows(n)
    send_weights(2)

    relays = []

    def relay(stage, which, ref):
        passed = []
        for n in crossing:
            at = sources[n] * CORES + core
            for i in which:
                weight_z[i, n].wait_recv()
            passed.append(
                remote(ref.at[at], ref.at[at], rs.at[stage, n], rr.at[stage, n], sibling)
            )
        ahead = which[-1] + 2
        if ahead < 3 + heads:
            send_weights(ahead)
        for i in which:
            own_local[i].wait()
            own_sibling[i].wait_recv()
        for copy in passed:
            copy.wait_recv()
        relays.extend(passed)

    for n in others:
        at = sources[n] * CORES + core
        ba_z[n - 1].wait_recv()
        relays.append(remote(ba.at[at], ba.at[at], brs.at[n], brr.at[n], sibling))
    for copy in later:
        copy.wait()
    for copy in [ba_own] + relays + seg_z:
        copy.wait_recv()
    relay(0, (0, 1), w_first)

    rows = seg.shape[2]
    holders, depth = ba.shape[0], ba.shape[2]
    model = tok.shape[3]
    row = lax.broadcasted_iota(jnp.int32, (rows, rows), 0)
    col = lax.broadcasted_iota(jnp.int32, (rows, rows), 1)
    lower = row >= col
    strict = row > col
    ones_lower = jnp.where(lower, 1.0, 0.0)
    lane = lax.broadcasted_iota(jnp.int32, (rows, count), 1)

    def project(first, slots, ref):
        left = tok[first : first + slots].reshape(slots * rows, model)
        right = ref[...].reshape(holders * depth, ref.shape[-1])
        result = jnp.dot(left, right, preferred_element_type=jnp.float32)
        return result.astype(jnp.bfloat16).astype(jnp.float32)

    tq = taps_q[:, columns(z, DK)]
    tk = taps_k[:, columns(z, DK)]
    tv = taps_v[:, columns(z, width)]
    inverse, outer, scores, betas, befores = [], [], [], [], []
    for first in range(0, nz, 2):
        for n in (first, first + 1):
            for copy in tok_y[n]:
                copy.wait_recv()
        pair = project(first, 2, w_first)
        left = tok[first : first + 2].reshape(2 * rows, model)
        small = jnp.zeros((2 * rows, 2 * count), jnp.float32)
        for s in range(holders):
            small = small + dot_rows(left[:, s * depth : (s + 1) * depth], ba[s])
        small = small.astype(jnp.bfloat16).astype(jnp.float32)
        lows = []
        for n in (first, first + 1):
            at = (n - first) * rows
            projected = pair[at : at + rows]
            beta_all = sigmoid(small[at : at + rows, :count])
            shifted = small[at : at + rows, count:] + bias[...]
            soft = jnp.maximum(shifted, 0.0) + jnp.log1p(jnp.exp(-jnp.abs(shifted)))
            cumulative = dot_exact(ones_lower, -rate[...] * soft)
            seg_row = jnp.broadcast_to(seg[n].astype(jnp.float32), (rows, rows))
            seg_col = seg_row.T
            same = seg_row == seg_col
            same_before = [
                (pltpu.roll(seg_col, offset, 0) == seg_col) & (row >= offset)
                for offset in range(1, 4)
            ]
            query = unit_rows(conv_rows(projected[:, :DK], tq, same_before)) * DK ** (-0.5)
            key = unit_rows(conv_rows(projected[:, DK:], tk, same_before))
            key_gram = product_rows(key, key)
            query_gram = product_rows(query, key)
            befores.append(same_before)
            for h in range(heads):
                pick = lane == z * heads + h
                beta = jnp.sum(jnp.where(pick, beta_all, 0.0), axis=1, keepdims=True)
                total = jnp.sum(jnp.where(pick, cumulative, 0.0), axis=1, keepdims=True)
                total = jnp.broadcast_to(total, (rows, rows))
                spread = jnp.where(lower, total - total.T, 0.0)
                decay = jnp.where(lower & same, jnp.exp(spread), 0.0)
                betas.append(beta)
                lows.append(jnp.where(strict, beta * key_gram * decay, 0.0))
                scores.append(query_gram * decay)
        blocks, rest = inverse_blocks(lows, row, col, rows)
        inverse += blocks
        outer += rest

    relay(1, (2,), w_second)
    rights = []
    projected = project(0, nz, w_second)
    for n in range(nz):
        values = conv_rows(projected[n * rows : (n + 1) * rows], tv, befores[n])
        for h in range(heads):
            rights.append(betas[n * heads + h] * values[:, h * DV : (h + 1) * DV])
    solved = [product(t, b) for t, b in zip(inverse, rights)]
    parts = [product(m, x) for m, x in zip(outer, solved)]
    solved = [x - product(t, p) for x, t, p in zip(solved, inverse, parts)]
    mixed = [product(s, x) for s, x in zip(scores, solved)]
    normed = [
        m * lax.rsqrt(jnp.mean(m * m, axis=-1, keepdims=True) + 1e-06) * out_gain[...]
        for m in mixed
    ]

    share = rows // ntp
    finals = []
    for h in range(heads):
        relay(2 + h, (3 + h,), w_third.at[h])
        place = columns((tp * nz + z) * heads + h, DV)
        gates = project(0, nz, w_third.at[h])
        for n in crossing + [0]:
            gate = gates[n * rows : (n + 1) * rows]
            tile = (normed[n * heads + h] * (gate * sigmoid(gate))).astype(jnp.bfloat16)
            for t in range(ntp):
                tiles[h, n, t] = tile[t * share : (t + 1) * share]
            for j in range(ntp):
                source = tiles.at[h, n, tp_at(j)]
                target = out.at[:, place]
                if n or j:
                    device = (sources[n] * CORES + core, tp_at(j))
                    finals.append(remote(source, target, cs.at[h, n, j], cr.at[h, n, j], device))
                else:
                    copy = pltpu.make_async_copy(source, target, cs.at[h, 0, 0])
                    copy.start()
                    finals.append(copy)
    for copy in list(tok_z.values()) + sum(tok_y.values(), []) + seg_z + ba_z + [ba_own]:
        copy.wait_send()
    for copy in list(weight_z.values()) + own_sibling + relays:
        copy.wait_send()
    for copy in finals:
        copy.wait()


def layer(n_dp, n_tp, *args):
    (
        tokens,
        norm_gain,
        w_query,
        w_key,
        w_value,
        w_gate,
        w_beta,
        w_decay,
        conv_query,
        conv_key,
        conv_value,
        decay_rate,
        dt_bias,
        out_gain,
        seg_ids,
    ) = args
    nz = n_dp // CORES
    rows = seg_ids.shape[1]
    share, model = tokens.shape
    depth = w_query.shape[0]
    value_heads = w_value.shape[1] // DV
    if n_dp % (2 * CORES) or w_query.shape[1] // DK != nz or value_heads % nz or rows != 128:
        return shards(*args)
    heads = value_heads // nz
    small = 2 * value_heads
    hbm = pl.BlockSpec(memory_space=pltpu.HBM)
    dma = pltpu.SemaphoreType.DMA
    one_row = norm_gain.reshape(1, -1), decay_rate.reshape(1, -1), dt_bias.reshape(1, -1)
    gain = out_gain.reshape(1, -1)
    narrow = w_beta.T, w_decay.T
    held = (tokens, one_row[0], *narrow, conv_query, conv_key, conv_value)
    held += one_row[1:] + (gain,)
    return pl.pallas_call(
        functools.partial(layer_kernel, nz, n_tp, heads),
        out_shape=jax.ShapeDtypeStruct((share, n_tp * value_heads * DV), jnp.bfloat16),
        in_specs=[hbm] * 15,
        out_specs=hbm,
        scratch_shapes=[pltpu.VMEM(a.shape, a.dtype) for a in held]
        + [
            pltpu.VMEM((nz, n_tp, share, model), jnp.bfloat16),
            pltpu.VMEM((n_dp, depth, 2 * DK), jnp.bfloat16),
            pltpu.VMEM((n_dp, depth, heads * DV), jnp.bfloat16),
            pltpu.VMEM((heads, n_dp, depth, DV), jnp.bfloat16),
            pltpu.VMEM((n_dp, small, depth), jnp.bfloat16),
            pltpu.VMEM((nz, 1, rows), jnp.int32),
            pltpu.VMEM((heads, nz, n_tp, share, DV), jnp.bfloat16),
            dma((11,)),
            dma((nz,)),
            dma((nz,)),
            dma((nz, n_tp)),
            dma((nz, n_tp)),
            dma((nz, 3 + heads)),
            dma((nz, 3 + heads)),
            dma((3 + heads,)),
            dma((3 + heads,)),
            dma((2 + heads, nz)),
            dma((2 + heads, nz)),
            dma((nz,)),
            dma((nz,)),
            dma((nz,)),
            dma((nz,)),
            dma((nz,)),
            dma((nz,)),
            dma((heads, nz, n_tp)),
            dma((heads, nz, n_tp)),
            dma((3 + heads,)),
        ],
        compiler_params=pltpu.CompilerParams(
            collective_id=0, has_side_effects=True, vmem_limit_bytes=60 * 2**20
        ),
    )(
        tokens,
        one_row[0],
        w_query,
        w_key,
        w_value,
        w_gate,
        *narrow,
        conv_query,
        conv_key,
        conv_value,
        one_row[1],
        one_row[2],
        gain,
        seg_ids,
    )


def solution(mesh):
    in_specs = (
        P(("dp", "tp"), None),
        P(),
        P("dp", "tp"),
        P("dp", "tp"),
        P("dp", "tp"),
        P("dp", "tp"),
        P("dp", "tp"),
        P("dp", "tp"),
        P(None, "tp"),
        P(None, "tp"),
        P(None, "tp"),
        P("tp"),
        P("tp"),
        P(),
        P("dp", None),
    )
    out_specs = P(("dp", "tp"), None)
    body = functools.partial(layer, mesh.shape["dp"], mesh.shape["tp"])
    return jax.shard_map(body, mesh=mesh, in_specs=in_specs, out_specs=out_specs, check_vma=False)
```

```python
import functools

import jax
import jax.numpy as jnp
from jax import lax
from jax.experimental import pallas as pl
from jax.experimental.pallas import tpu as pltpu
from jax.sharding import PartitionSpec as P

DK = 128
DV = 128
SPAN = 64


highest = lax.Precision.HIGHEST


def rms_rows(tokens, gain):
    floats = tokens.astype(jnp.float32)
    scaled = floats * lax.rsqrt(jnp.mean(floats * floats, axis=-1, keepdims=True) + 1e-06)
    return (scaled * gain).astype(jnp.bfloat16)


def split_columns(projected, column_counts):
    pieces = []
    offset = 0
    for count in column_counts:
        pieces.append(projected[:, offset : offset + count])
        offset = offset + count
    return pieces


def causal_conv(projected, kernel, segment):
    kernel_len = kernel.shape[0]
    summed = projected * kernel[kernel_len - 1]
    for offset in range(1, kernel_len):
        zeros_top = jnp.zeros((offset, projected.shape[1]), jnp.float32)
        shifted = jnp.concatenate([zeros_top, projected[:-offset]], axis=0)
        earlier = jnp.concatenate([jnp.full((offset,), -1, jnp.int32), segment[:-offset]])
        same_doc = (earlier == segment).astype(jnp.float32)
        summed = summed + shifted * same_doc[:, None] * kernel[kernel_len - 1 - offset]
    return jax.nn.silu(summed)


def unit_heads(values, heads, head_size):
    shaped = values.reshape(values.shape[0], heads, head_size)
    return shaped * lax.rsqrt(jnp.sum(shaped * shaped, axis=-1, keepdims=True) + 1e-06)


def delta_head(query, key_rows, value, beta, log_decay, segment):
    row_count = query.shape[0]
    blocks = row_count // SPAN
    value_size = value.shape[1]
    q_blocks = query.reshape(blocks, SPAN, query.shape[1])
    k_blocks = key_rows.reshape(blocks, SPAN, key_rows.shape[1])
    v_blocks = value.reshape(blocks, SPAN, value_size)
    beta_blocks = beta.reshape(blocks, SPAN)
    decay_blocks = log_decay.reshape(blocks, SPAN)
    seg_blocks = segment.reshape(blocks, SPAN)
    before = jnp.concatenate([jnp.full((1,), -1, jnp.int32), seg_blocks[:-1, -1]])
    row_index = lax.broadcasted_iota(jnp.int32, (SPAN, SPAN), 0)
    col_index = lax.broadcasted_iota(jnp.int32, (SPAN, SPAN), 1)
    lower_mask = row_index >= col_index
    strict = row_index > col_index

    def advance(state, inputs):
        block_q, block_k, block_v, block_beta, block_decay, block_seg, block_before = inputs
        cumulative = jnp.cumsum(block_decay)
        same_doc = block_seg[:, None] == block_seg[None, :]
        spread = jnp.where(lower_mask, cumulative[:, None] - cumulative[None, :], 0.0)
        decay_matrix = jnp.where(lower_mask & same_doc, jnp.exp(spread), 0.0)
        carried = (block_seg == block_before).astype(jnp.float32)
        from_start = jnp.exp(cumulative) * carried
        key_gram = jnp.dot(block_k, block_k.T, precision=highest)
        lower_matrix = jnp.where(strict, block_beta[:, None] * key_gram * decay_matrix, 0.0)
        system = jnp.eye(SPAN, dtype=jnp.float32) + lower_matrix
        right_side = jnp.concatenate(
            [block_beta[:, None] * block_v, (block_beta * from_start)[:, None] * block_k], axis=1
        )
        solved = lax.linalg.triangular_solve(
            system, right_side, left_side=True, lower=True, unit_diagonal=True
        )
        updates = solved[:, :value_size] - jnp.dot(solved[:, value_size:], state, precision=highest)
        scores = jnp.dot(block_q, block_k.T, precision=highest) * decay_matrix
        output = jnp.dot(from_start[:, None] * block_q, state, precision=highest) + jnp.dot(
            scores, updates, precision=highest
        )
        tail_weight = jnp.where(
            block_seg == block_seg[-1], jnp.exp(cumulative[-1] - cumulative), 0.0
        )
        new_state = jnp.exp(cumulative[-1]) * carried[-1] * state + jnp.dot(
            (tail_weight[:, None] * block_k).T, updates, precision=highest
        )
        return (new_state, output)

    initial = jnp.zeros((key_rows.shape[1], value_size), jnp.float32)
    last_state, outputs = lax.scan(
        advance,
        initial,
        (q_blocks, k_blocks, v_blocks, beta_blocks, decay_blocks, seg_blocks, before),
    )
    return outputs.reshape(row_count, value_size)


def prepare_heads(parts, segment, conv_query, conv_key, conv_value, decay_rate, dt_bias):
    proj_query, proj_key, proj_value, proj_gate, proj_beta, proj_decay = [
        piece_part.astype(jnp.float32) for piece_part in parts
    ]
    key_heads = proj_query.shape[1] // DK
    value_heads = proj_value.shape[1] // DV
    repeat = value_heads // key_heads
    query = unit_heads(causal_conv(proj_query, conv_query, segment), key_heads, DK) * DK ** (-0.5)
    keys = unit_heads(causal_conv(proj_key, conv_key, segment), key_heads, DK)
    values = causal_conv(proj_value, conv_value, segment).reshape(
        proj_value.shape[0], value_heads, DV
    )
    query = jnp.repeat(query, repeat, axis=1)
    keys = jnp.repeat(keys, repeat, axis=1)
    beta = jax.nn.sigmoid(proj_beta)
    log_decay = -decay_rate * jax.nn.softplus(proj_decay + dt_bias)
    gate_act = jax.nn.silu(proj_gate.reshape(proj_gate.shape[0], value_heads, DV))
    return (query, keys, values, beta, log_decay, gate_act)


def finish_heads(mixed, gate_act, out_gain):
    normed = mixed * lax.rsqrt(jnp.mean(mixed * mixed, axis=-1, keepdims=True) + 1e-06) * out_gain
    return (normed * gate_act).astype(jnp.bfloat16)


def shards(
    tokens,
    norm_gain,
    w_query,
    w_key,
    w_value,
    w_gate,
    w_beta,
    w_decay,
    conv_query,
    conv_key,
    conv_value,
    decay_rate,
    dt_bias,
    out_gain,
    seg_ids,
):
    gathered = (
        lax.all_gather(w_query, "dp", axis=0, tiled=True),
        lax.all_gather(w_key, "dp", axis=0, tiled=True),
        lax.all_gather(w_value, "dp", axis=0, tiled=True),
        lax.all_gather(w_gate, "dp", axis=0, tiled=True),
        lax.all_gather(w_beta, "dp", axis=0, tiled=True),
        lax.all_gather(w_decay, "dp", axis=0, tiled=True),
    )
    column_counts = [matrix.shape[1] for matrix in gathered]
    joined = jnp.concatenate(gathered, axis=1)
    projected = jnp.dot(
        rms_rows(lax.all_gather(tokens, "tp", axis=0, tiled=True), norm_gain),
        joined,
        preferred_element_type=jnp.float32,
    ).astype(jnp.bfloat16)
    parts = split_columns(projected, column_counts)
    segment = seg_ids[0]
    query, keys, values, beta, log_decay, gate_act = prepare_heads(
        parts, segment, conv_query, conv_key, conv_value, decay_rate, dt_bias
    )
    row_count = values.shape[0]
    local_heads = values.shape[1]
    mixed = jax.vmap(delta_head, in_axes=(1, 1, 1, 1, 1, None), out_axes=1)(
        query, keys, values, beta, log_decay, segment
    )
    tiles = finish_heads(mixed, gate_act, out_gain).reshape(row_count, local_heads * DV)
    return lax.all_to_all(tiles, "tp", split_axis=0, concat_axis=1, tiled=True)


MESH = pl.DeviceIdType.MESH
CORES = 2
STEP = 8


def dot_exact(left, right):
    return jnp.dot(left, right, precision=highest, preferred_element_type=jnp.float32)


def dot_rows(left, right, precision=None):
    return lax.dot_general(
        left,
        right,
        (((1,), (1,)), ((), ())),
        precision=precision,
        preferred_element_type=jnp.float32,
    )


def two_parts(values):
    high = values.astype(jnp.bfloat16)
    low = (values - high.astype(jnp.float32)).astype(jnp.bfloat16)
    return high, low


def product(left, right):
    left_parts = jnp.concatenate(two_parts(left), axis=1)
    right_parts = jnp.concatenate(two_parts(right), axis=1)
    right_parts = jnp.concatenate([right_parts, right_parts], axis=0)
    both = jnp.dot(left_parts, right_parts, preferred_element_type=jnp.float32)
    size = right.shape[1]
    return both[:, :size] + both[:, size:]


def product_rows(left, right):
    left_parts = jnp.concatenate(two_parts(left), axis=1)
    right_parts = jnp.concatenate(two_parts(right), axis=0)
    right_parts = jnp.concatenate([right_parts, right_parts], axis=1)
    both = dot_rows(left_parts, right_parts)
    size = right.shape[0]
    return both[:, :size] + both[:, size:]


def sigmoid(x):
    return 1.0 / (1.0 + jnp.exp(-x))


def unit_rows(values):
    return values * lax.rsqrt(jnp.sum(values * values, axis=-1, keepdims=True) + 1e-06)


def conv_rows(projected, taps, same_before):
    summed = projected * taps[3:4]
    for offset in range(1, 4):
        shifted = pltpu.roll(projected, offset, 0)
        mask = same_before[offset - 1]
        if projected.shape[1] > mask.shape[1]:
            mask = jnp.concatenate([mask] * (projected.shape[1] // mask.shape[1]), axis=1)
        summed = summed + jnp.where(mask, shifted, 0.0) * taps[3 - offset : 4 - offset]
    return summed * sigmoid(summed)


def inverse_blocks(lows, row, col, rows):
    eye = jnp.where(row == col, 1.0, 0.0)

    def block(size):
        return row // size == col // size

    inner = [jnp.where(block(STEP), m, 0.0) for m in lows]
    squares = [product(m, m) for m in inner]
    fourths = [product(m, m) for m in squares]
    firsts = [eye - m + s - product(m, s) for m, s in zip(inner, squares)]
    inverse = [f + product(f, q) for f, q in zip(firsts, fourths)]
    size = STEP
    while size < rows // 4:
        ring = block(2 * size) & jnp.logical_not(block(size))
        parts = [product(jnp.where(ring, m, 0.0), t) for m, t in zip(lows, inverse)]
        inverse = [t - product(t, p) for t, p in zip(inverse, parts)]
        size = 2 * size
    outer = jnp.logical_not(block(size))
    return inverse, [jnp.where(outer, m, 0.0) for m in lows]


def layer_kernel(
    nz,
    ntp,
    heads,
    tokens_hbm,
    gain_hbm,
    w_query,
    w_key,
    w_value,
    w_gate,
    beta_hbm,
    decay_hbm,
    taps_q_hbm,
    taps_k_hbm,
    taps_v_hbm,
    rate_hbm,
    bias_hbm,
    out_gain_hbm,
    seg_hbm,
    out,
    tokens,
    norm_gain,
    w_beta,
    w_decay,
    taps_q,
    taps_k,
    taps_v,
    rate,
    bias,
    out_gain,
    tok,
    w_first,
    w_second,
    w_third,
    ba,
    seg,
    tiles,
    loads,
    zs,
    zr,
    ys,
    yr,
    ws,
    wr,
    os,
    orr,
    rs,
    rr,
    bs,
    br,
    brs,
    brr,
    ss,
    sr,
    cs,
    cr,
    local,
):
    dp = lax.axis_index("dp")
    tp = lax.axis_index("tp")
    z = dp // CORES
    core = dp % CORES
    sibling = (z * CORES + 1 - core, tp)
    width = heads * DV

    def z_at(k):
        return lax.rem(z + k, nz)

    def dp_at(k):
        return z_at(k) * CORES + core

    def tp_at(j):
        return lax.rem(tp + j, ntp)

    def remote(source, target, send, recv, device):
        copy = pltpu.make_async_remote_copy(
            src_ref=source,
            dst_ref=target,
            send_sem=send,
            recv_sem=recv,
            device_id=device,
            device_id_type=MESH,
        )
        copy.start()
        return copy

    def load(i, source, target):
        copy = pltpu.make_async_copy(source, target, loads.at[i])
        copy.start()
        return copy

    early = [
        load(0, tokens_hbm, tokens),
        load(1, gain_hbm, norm_gain),
        load(2, beta_hbm, w_beta),
        load(3, decay_hbm, w_decay),
        load(4, seg_hbm, seg.at[0]),
    ]
    later = [
        load(5, taps_q_hbm, taps_q),
        load(6, taps_k_hbm, taps_k),
        load(7, taps_v_hbm, taps_v),
        load(8, rate_hbm, rate),
        load(9, bias_hbm, bias),
        load(10, out_gain_hbm, out_gain),
    ]

    barrier = pltpu.get_barrier_semaphore()
    for k in range(nz):
        for j in range(ntp):
            if k or j:
                pl.semaphore_signal(
                    barrier, inc=1, device_id=(dp_at(k), tp_at(j)), device_id_type=MESH
                )
    pl.semaphore_signal(barrier, inc=1, device_id=sibling, device_id_type=MESH)

    def columns(chip, size):
        return pl.ds(pl.multiple_of(chip * size, size), size)

    def pieces(chip):
        return (
            (w_query.at[:, columns(chip, DK)], w_first.at[dp, :, 0:DK]),
            (w_key.at[:, columns(chip, DK)], w_first.at[dp, :, DK : 2 * DK]),
            (w_value.at[:, columns(chip, width)], w_second.at[dp]),
        ) + tuple(
            (w_gate.at[:, columns(chip * heads + h, DV)], w_third.at[h, dp]) for h in range(heads)
        )

    for copy in early:
        copy.wait()
    own_local = []
    for i, (source, target) in enumerate(pieces(z)):
        copy = pltpu.make_async_copy(source, target, local.at[i])
        copy.start()
        own_local.append(copy)

    floats = tokens[...].astype(jnp.float32)
    scaled = floats * lax.rsqrt(jnp.mean(floats * floats, axis=-1, keepdims=True) + 1e-06)
    tok[0, tp] = (scaled * norm_gain[...]).astype(jnp.bfloat16)
    count = w_beta.shape[0]
    narrow = [w_beta[...].astype(jnp.float32), w_decay[...].astype(jnp.float32)]
    ba[dp] = jnp.concatenate(narrow, axis=0).astype(jnp.bfloat16)

    pl.semaphore_wait(barrier, nz * ntp)

    half = nz // 2
    base = (z // half) * half
    mirror = lax.rem(z + half, nz)
    targets = [z, mirror]
    sources = [z, mirror]
    for k in range(1, half):
        ahead = base + lax.rem(z + k, half)
        behind = base + lax.rem(z + half - k, half)
        targets += [ahead, lax.rem(ahead + half, nz)]
        sources += [behind, lax.rem(behind + half, nz)]
    others = range(1, nz)
    evens = range(2, nz, 2)
    crossing = list(range(1, nz, 2)) + list(evens)

    def device_of(chip):
        return (chip * CORES + core, tp)

    def send_rows(source, slot):
        return remote(
            tok.at[source, tp],
            tok.at[slot, tp],
            zs.at[slot],
            zr.at[slot],
            device_of(targets[slot - source]),
        )

    def spread_rows(slot):
        return [
            remote(
                tok.at[slot, tp], tok.at[slot, tp], ys.at[slot, j], yr.at[slot, j], (dp, tp_at(j))
            )
            for j in range(1, ntp)
        ]

    tok_z = {1: send_rows(0, 1)}
    for n in evens:
        tok_z[n] = send_rows(0, n)
    tok_y = {0: spread_rows(0)}
    seg_z = []
    ba_z = []
    for n in others:
        peer = device_of(targets[n])
        seg_z.append(remote(seg.at[0], seg.at[n], ss.at[n], sr.at[n], peer))
        ba_z.append(remote(ba.at[dp], ba.at[dp], bs.at[n], br.at[n], peer))

    weight_z = {}

    def send_weights(i):
        for n in crossing:
            source, target = pieces(targets[n])[i]
            weight_z[i, n] = remote(
                source, target, ws.at[n, i], wr.at[n, i], device_of(targets[n])
            )

    send_weights(0)
    send_weights(1)
    tok_z[1].wait_recv()
    for n in evens:
        tok_z[n + 1] = send_rows(1, n + 1)
    tok_y[1] = spread_rows(1)
    own_sibling = []
    for i, (source, target) in enumerate(pieces(z)):
        own_sibling.append(remote(source, target, os.at[i], orr.at[i], sibling))
    ba_own = remote(ba.at[dp], ba.at[dp], brs.at[0], brr.at[0], sibling)
    for n in range(2, nz):
        tok_z[n].wait_recv()
        tok_y[n] = spread_rows(n)
    for i in range(2, 3 + heads):
        send_weights(i)

    relays = []

    def relay(stage, which, ref):
        passed = []
        for n in crossing:
            at = sources[n] * CORES + core
            for i in which:
                weight_z[i, n].wait_recv()
            passed.append(
                remote(ref.at[at], ref.at[at], rs.at[stage, n], rr.at[stage, n], sibling)
            )
        for i in which:
            own_local[i].wait()
            own_sibling[i].wait_recv()
        for copy in passed:
            copy.wait_recv()
        relays.extend(passed)

    for n in others:
        at = sources[n] * CORES + core
        ba_z[n - 1].wait_recv()
        relays.append(remote(ba.at[at], ba.at[at], brs.at[n], brr.at[n], sibling))
    for copy in later:
        copy.wait()
    for copy in [ba_own] + relays + seg_z:
        copy.wait_recv()
    relay(0, (0, 1), w_first)

    rows = seg.shape[2]
    holders, depth = ba.shape[0], ba.shape[2]
    model = tok.shape[3]
    row = lax.broadcasted_iota(jnp.int32, (rows, rows), 0)
    col = lax.broadcasted_iota(jnp.int32, (rows, rows), 1)
    lower = row >= col
    strict = row > col
    ones_lower = jnp.where(lower, 1.0, 0.0)
    lane = lax.broadcasted_iota(jnp.int32, (rows, count), 1)

    def project(first, slots, ref):
        left = tok[first : first + slots].reshape(slots * rows, model)
        right = ref[...].reshape(holders * depth, ref.shape[-1])
        result = jnp.dot(left, right, preferred_element_type=jnp.float32)
        return result.astype(jnp.bfloat16).astype(jnp.float32)

    tq = taps_q[:, columns(z, DK)]
    tk = taps_k[:, columns(z, DK)]
    tv = taps_v[:, columns(z, width)]
    inverse, outer, scores, betas, befores = [], [], [], [], []
    for first in range(0, nz, 2):
        for n in (first, first + 1):
            for copy in tok_y[n]:
                copy.wait_recv()
        pair = project(first, 2, w_first)
        left = tok[first : first + 2].reshape(2 * rows, model)
        small = jnp.zeros((2 * rows, 2 * count), jnp.float32)
        for s in range(holders):
            small = small + dot_rows(left[:, s * depth : (s + 1) * depth], ba[s])
        small = small.astype(jnp.bfloat16).astype(jnp.float32)
        lows = []
        for n in (first, first + 1):
            at = (n - first) * rows
            projected = pair[at : at + rows]
            beta_all = sigmoid(small[at : at + rows, :count])
            shifted = small[at : at + rows, count:] + bias[...]
            soft = jnp.maximum(shifted, 0.0) + jnp.log1p(jnp.exp(-jnp.abs(shifted)))
            cumulative = dot_exact(ones_lower, -rate[...] * soft)
            seg_row = jnp.broadcast_to(seg[n].astype(jnp.float32), (rows, rows))
            seg_col = seg_row.T
            same = seg_row == seg_col
            same_before = [
                (pltpu.roll(seg_col, offset, 0) == seg_col) & (row >= offset)
                for offset in range(1, 4)
            ]
            query = unit_rows(conv_rows(projected[:, :DK], tq, same_before)) * DK ** (-0.5)
            key = unit_rows(conv_rows(projected[:, DK:], tk, same_before))
            key_gram = product_rows(key, key)
            query_gram = product_rows(query, key)
            befores.append(same_before)
            for h in range(heads):
                pick = lane == z * heads + h
                beta = jnp.sum(jnp.where(pick, beta_all, 0.0), axis=1, keepdims=True)
                total = jnp.sum(jnp.where(pick, cumulative, 0.0), axis=1, keepdims=True)
                total = jnp.broadcast_to(total, (rows, rows))
                spread = jnp.where(lower, total - total.T, 0.0)
                decay = jnp.where(lower & same, jnp.exp(spread), 0.0)
                betas.append(beta)
                lows.append(jnp.where(strict, beta * key_gram * decay, 0.0))
                scores.append(query_gram * decay)
        blocks, rest = inverse_blocks(lows, row, col, rows)
        inverse += blocks
        outer += rest

    relay(1, (2,), w_second)
    rights = []
    projected = project(0, nz, w_second)
    for n in range(nz):
        values = conv_rows(projected[n * rows : (n + 1) * rows], tv, befores[n])
        for h in range(heads):
            rights.append(betas[n * heads + h] * values[:, h * DV : (h + 1) * DV])
    solved = [product(t, b) for t, b in zip(inverse, rights)]
    parts = [product(m, x) for m, x in zip(outer, solved)]
    solved = [x - product(t, p) for x, t, p in zip(solved, inverse, parts)]
    mixed = [product(s, x) for s, x in zip(scores, solved)]
    normed = [
        m * lax.rsqrt(jnp.mean(m * m, axis=-1, keepdims=True) + 1e-06) * out_gain[...]
        for m in mixed
    ]

    share = rows // ntp
    finals = []
    for h in range(heads):
        relay(2 + h, (3 + h,), w_third.at[h])
        place = columns((tp * nz + z) * heads + h, DV)
        gates = project(0, nz, w_third.at[h])
        for n in crossing + [0]:
            gate = gates[n * rows : (n + 1) * rows]
            tile = (normed[n * heads + h] * (gate * sigmoid(gate))).astype(jnp.bfloat16)
            for t in range(ntp):
                tiles[h, n, t] = tile[t * share : (t + 1) * share]
            for j in range(ntp):
                source = tiles.at[h, n, tp_at(j)]
                target = out.at[:, place]
                if n or j:
                    device = (sources[n] * CORES + core, tp_at(j))
                    finals.append(remote(source, target, cs.at[h, n, j], cr.at[h, n, j], device))
                else:
                    copy = pltpu.make_async_copy(source, target, cs.at[h, 0, 0])
                    copy.start()
                    finals.append(copy)
    for copy in list(tok_z.values()) + sum(tok_y.values(), []) + seg_z + ba_z + [ba_own]:
        copy.wait_send()
    for copy in list(weight_z.values()) + own_sibling + relays:
        copy.wait_send()
    for copy in finals:
        copy.wait()


def layer(n_dp, n_tp, *args):
    (
        tokens,
        norm_gain,
        w_query,
        w_key,
        w_value,
        w_gate,
        w_beta,
        w_decay,
        conv_query,
        conv_key,
        conv_value,
        decay_rate,
        dt_bias,
        out_gain,
        seg_ids,
    ) = args
    nz = n_dp // CORES
    rows = seg_ids.shape[1]
    share, model = tokens.shape
    depth = w_query.shape[0]
    value_heads = w_value.shape[1] // DV
    if n_dp % (2 * CORES) or w_query.shape[1] // DK != nz or value_heads % nz or rows != 128:
        return shards(*args)
    heads = value_heads // nz
    small = 2 * value_heads
    hbm = pl.BlockSpec(memory_space=pltpu.HBM)
    dma = pltpu.SemaphoreType.DMA
    one_row = norm_gain.reshape(1, -1), decay_rate.reshape(1, -1), dt_bias.reshape(1, -1)
    gain = out_gain.reshape(1, -1)
    narrow = w_beta.T, w_decay.T
    held = (tokens, one_row[0], *narrow, conv_query, conv_key, conv_value)
    held += one_row[1:] + (gain,)
    return pl.pallas_call(
        functools.partial(layer_kernel, nz, n_tp, heads),
        out_shape=jax.ShapeDtypeStruct((share, n_tp * value_heads * DV), jnp.bfloat16),
        in_specs=[hbm] * 15,
        out_specs=hbm,
        scratch_shapes=[pltpu.VMEM(a.shape, a.dtype) for a in held]
        + [
            pltpu.VMEM((nz, n_tp, share, model), jnp.bfloat16),
            pltpu.VMEM((n_dp, depth, 2 * DK), jnp.bfloat16),
            pltpu.VMEM((n_dp, depth, heads * DV), jnp.bfloat16),
            pltpu.VMEM((heads, n_dp, depth, DV), jnp.bfloat16),
            pltpu.VMEM((n_dp, small, depth), jnp.bfloat16),
            pltpu.VMEM((nz, 1, rows), jnp.int32),
            pltpu.VMEM((heads, nz, n_tp, share, DV), jnp.bfloat16),
            dma((11,)),
            dma((nz,)),
            dma((nz,)),
            dma((nz, n_tp)),
            dma((nz, n_tp)),
            dma((nz, 3 + heads)),
            dma((nz, 3 + heads)),
            dma((3 + heads,)),
            dma((3 + heads,)),
            dma((2 + heads, nz)),
            dma((2 + heads, nz)),
            dma((nz,)),
            dma((nz,)),
            dma((nz,)),
            dma((nz,)),
            dma((nz,)),
            dma((nz,)),
            dma((heads, nz, n_tp)),
            dma((heads, nz, n_tp)),
            dma((3 + heads,)),
        ],
        compiler_params=pltpu.CompilerParams(
            collective_id=0, has_side_effects=True, vmem_limit_bytes=60 * 2**20
        ),
    )(
        tokens,
        one_row[0],
        w_query,
        w_key,
        w_value,
        w_gate,
        *narrow,
        conv_query,
        conv_key,
        conv_value,
        one_row[1],
        one_row[2],
        gain,
        seg_ids,
    )


def solution(mesh):
    in_specs = (
        P(("dp", "tp"), None),
        P(),
        P("dp", "tp"),
        P("dp", "tp"),
        P("dp", "tp"),
        P("dp", "tp"),
        P("dp", "tp"),
        P("dp", "tp"),
        P(None, "tp"),
        P(None, "tp"),
        P(None, "tp"),
        P("tp"),
        P("tp"),
        P(),
        P("dp", None),
    )
    out_specs = P(("dp", "tp"), None)
    body = functools.partial(layer, mesh.shape["dp"], mesh.shape["tp"])
    return jax.shard_map(body, mesh=mesh, in_specs=in_specs, out_specs=out_specs, check_vma=False)
```
